768 devices in a mesh: grid: 48 (over z, y_lo, core), tp: 16 (over x, y_hi).
Axes of the slice: x: 4, y: 8 (y_hi: 4, y_lo: 2; y = y_hi * 2 + y_lo), z: 12, core: 2. Of those that a mesh axis runs over, the one named last changes fastest.
Arguments:
- latents: bfloat16 [18432, 3072], P('grid'), may hold values from -6 to 6
- input_weight: bfloat16 [3072, 6144], P('grid', 'tp'), as said below
- norm_gains: float32 [2, 128], replicated, as said below
- text_pairs: bfloat16 [256, 4096], P(None, 'tp'), may hold values from -6 to 6
- text_count: int32 [1], replicated, may hold values from 64 to 256
- output_weight: bfloat16 [2048, 3072], P('tp', 'grid'), may hold values from -0.125 to 0.125
Outputs:
- block_output: bfloat16 [18432, 3072], P('grid', 'tp')
The draws below stay inside these ranges and needn't reach their ends.
Inputs may be any that keep to these rules, and one draw needn't show every extreme that they name: `text_count`: number of valid text tokens; the remaining text slots are padding. `input_weight`: a projection scaled by its fan-in. `norm_gains`: positive gains.
All inputs are finite; a program needn't handle non-finite values.
Results may differ from the reference program's by a relative error of at most 0.015.
Values may be sent and summed in bfloat16 or wider, within the bound.
A program may use at most 32 MiB of HBM per device.

```python
import jax
import jax.numpy as jnp
import numpy as np
from jax import lax

D = 3072
HD = 128
TXT = 256
HEAD_DEV = 1
GRID_H = 4
WT = 1
TILE = 384
HEADS = 16
TOKENS = 18432
N_TP = 16


def draw_input_weight(key, part):
    first_key = jax.random.fold_in(key, 11)
    basis = jax.random.normal(first_key, (D, HEADS, 3, HD), jnp.float32) * D ** (-0.5)
    return basis.reshape(D, 3 * HEADS * HD).astype(jnp.bfloat16)


def draw_norm_gains(key, part):
    gain_key = jax.random.fold_in(key, 21)
    return jax.random.uniform(gain_key, (2, HD), jnp.float32, 0.6, 1.6)


def levels(rng, shape, shards, smallest, largest):
    level, own = 1.0, jax.random.fold_in(rng, 6)
    for axis_at, parts in shards:
        heights = jnp.exp(jax.random.uniform(jax.random.fold_in(own, axis_at), (parts,), jnp.float32, smallest / len(shards), largest / len(shards)))
        level = level * jnp.repeat(heights, shape[axis_at] // parts).reshape([-1 if axis == axis_at else 1 for axis in range(len(shape))])
    return level


def centred(rng, extent, spread, bound, shards=(), kind=jnp.bfloat16):
    factor_of = levels(rng, extent, shards, -0.22, 0.18) if shards else 1.0
    entries = jax.random.normal(rng, extent, jnp.float32) * spread * factor_of
    return jnp.minimum(jnp.maximum(entries, -bound), bound).astype(kind)


def setup_inputs(seed: int = 0) -> dict:
    keys = jax.random.split(jax.random.key(seed), 7)
    latents = centred(keys[0], (TOKENS, D), 1.0, 6.0, ((0, 48),))
    input_weight = draw_input_weight(jax.random.fold_in(keys[6], 71), 0)
    norm_gains = draw_norm_gains(jax.random.fold_in(keys[6], 71), 0)
    text_pairs = centred(keys[3], (TXT, 2 * HEADS * HD), 1.0, 6.0, ((1, 16),))
    text_count = jax.random.randint(keys[4], (1,), TXT // 4, TXT + 1).astype(jnp.int32)
    output_weight = centred(keys[5], (HEADS * HD, D), (HEADS * HD) ** -0.5, 0.125, ((0, 16), (1, 48)))
    return dict(latents=latents, input_weight=input_weight, norm_gains=norm_gains, text_pairs=text_pairs, text_count=text_count, output_weight=output_weight)


epsilon = 1e-06

def root_norm(values, gain):
    return values * lax.rsqrt(lax.optimization_barrier(jnp.mean(values * values, axis=-1, keepdims=True)) + epsilon) * gain

def reference(latents, input_weight, norm_gains, text_pairs, text_count, output_weight):
    projected = jnp.dot(latents, input_weight, preferred_element_type=jnp.float32).reshape(TOKENS, HEADS, 3, HD)
    queries = root_norm(projected[:, :, 0], norm_gains[0]).astype(jnp.bfloat16)
    key_rows = root_norm(projected[:, :, 1], norm_gains[1]).astype(jnp.bfloat16)
    values = projected[:, :, 2].astype(jnp.bfloat16)
    text = text_pairs.reshape(TXT, HEADS, 2, HD)
    text_keys = root_norm(text[:, :, 0].astype(jnp.float32), norm_gains[1]).astype(jnp.bfloat16)
    text_values = text[:, :, 1]
    grid_time = TOKENS // (TILE * GRID_H * WT)
    width_keep = min(3, WT)
    starts = np.clip(np.arange(WT) - 1, 0, WT - width_keep)
    width_index = starts[:, None] + np.arange(width_keep)[None, :]
    width_ok = np.abs(width_index - np.arange(WT)[:, None]) <= 1
    offsets = [(step_time, step_height) for step_time in (-1, 0, 1) for step_height in (-1, 0, 1)]
    time_pos = jnp.arange(grid_time)
    height_pos = jnp.arange(GRID_H)
    plane_ok = jnp.stack([(time_pos[:, None] + step_time >= 0) & (time_pos[:, None] + step_time < grid_time) & ((height_pos[None, :] + step_height >= 0) & (height_pos[None, :] + step_height < GRID_H)) for step_time, step_height in offsets])
    live = plane_ok[:, :, :, None, None, None] & jnp.asarray(width_ok)[None, None, None, :, :, None]
    live = jnp.broadcast_to(live, (9, grid_time, GRID_H, WT, width_keep, TILE))
    live = live.transpose(1, 2, 3, 0, 4, 5).reshape(grid_time, GRID_H, WT, 9 * width_keep * TILE)
    live_text = jnp.arange(TXT) < text_count[0]
    score_scale = HD ** (-0.5)

    def windows(rows):
        tiles = rows.reshape(grid_time, GRID_H, WT, TILE, HD)
        padded = jnp.pad(tiles, ((1, 1), (1, 1), (0, 0), (0, 0), (0, 0)))
        stacked = jnp.stack([padded[1 + step_time:1 + step_time + grid_time, 1 + step_height:1 + step_height + GRID_H] for step_time, step_height in offsets])
        chosen = stacked[:, :, :, width_index]
        return chosen.transpose(1, 2, 3, 0, 4, 5, 6).reshape(grid_time, GRID_H, WT, 9 * width_keep * TILE, HD).astype(jnp.float32)

    def one_head(operands):
        query_head, key_head, value_head, text_key, text_value = operands
        query_tiles = query_head.reshape(grid_time, GRID_H, WT, TILE, HD).astype(jnp.float32)
        key_window = windows(key_head)
        value_window = windows(value_head)
        video_scores = jnp.einsum('abwqd,abwkd->abwqk', query_tiles, key_window) * score_scale
        text_scores = jnp.einsum('abwqd,kd->abwqk', query_tiles, text_key.astype(jnp.float32)) * score_scale
        video_scores = jnp.where(live[:, :, :, None, :], video_scores, -jnp.inf)
        text_scores = jnp.where(live_text[None, None, None, None, :], text_scores, -jnp.inf)
        row_max = jnp.maximum(video_scores.max(-1), text_scores.max(-1))[..., None]
        video_exp = jnp.exp(video_scores - row_max)
        text_exp = jnp.exp(text_scores - row_max)
        denominator = video_exp.sum(-1, keepdims=True) + text_exp.sum(-1, keepdims=True)
        video_weights = (video_exp / denominator).astype(jnp.bfloat16)
        text_weights = (text_exp / denominator).astype(jnp.bfloat16)
        mixed = jnp.einsum('abwqk,abwkd->abwqd', video_weights.astype(jnp.float32), value_window)
        mixed = mixed + jnp.einsum('abwqk,kd->abwqd', text_weights.astype(jnp.float32), text_value.astype(jnp.float32))
        return mixed.astype(jnp.bfloat16).reshape(TOKENS, HD)
    per_head = lax.map(one_head, (queries.transpose(1, 0, 2), key_rows.transpose(1, 0, 2), values.transpose(1, 0, 2), text_keys.transpose(1, 0, 2), text_values.transpose(1, 0, 2)))
    attention = per_head.transpose(1, 0, 2).reshape(TOKENS, HEADS * HD)
    group_width = HEAD_DEV * HD
    summed = jnp.zeros((TOKENS, D), jnp.float32)
    for group in range(N_TP):
        partial_term = jnp.dot(attention[:, group * group_width:(group + 1) * group_width], output_weight[group * group_width:(group + 1) * group_width], preferred_element_type=jnp.float32).astype(jnp.bfloat16)
        partial_term = lax.optimization_barrier(partial_term)
        summed = summed + partial_term.astype(jnp.float32)
    return summed.astype(jnp.bfloat16)
```

```python
import functools

import jax
import jax.numpy as jnp
from jax import lax
from jax.experimental import pallas as pl
from jax.experimental.pallas import tpu as pltpu
from jax.sharding import PartitionSpec as P

NZ = 12
NX = 4
NYH = 4
TILE = 384
HD = 128
RANK = 64
BLOCKS = 3
ROWS = TILE // BLOCKS
OUT = 192
EPS = 1e-6
MESH = pl.DeviceIdType.MESH
NT = (((1,), (1,)), ((), ()))
F32 = jnp.float32
BF16 = jnp.bfloat16


def rms(values, gain):
    return values * lax.rsqrt(jnp.mean(values * values, axis=-1, keepdims=True) + EPS) * gain


def chunks_of(step):
    if step == 0:
        return [0]
    if step == NZ // 2:
        return [NZ - 1]
    return [2 * step - 1, 2 * step]


def kernel(
    lat_hbm, win_hbm, gains, text, count, wout_hbm, out,
    lat, w, w2, piece, acc, q, kv, m, l, o, att, part, send, got,
    local_sem, perm_sem,
    wz_s, wz_r, wy_s, wy_r, wc_s, wc_r,
    vz_s, vz_r, vy_s, vy_r, vc_s, vc_r,
    kz_s, kz_r, ky_s, ky_r, kc_s, kc_r,
    at_s, at_r, rs_s, rs_r,
):
    g = lax.axis_index("grid")
    t = lax.axis_index("tp")
    z, yl, c = g // 4, (g // 2) % 2, g % 2
    x, yh = t // NYH, t % NYH
    inner = yl + c == 1

    def mod(value, n):
        return lax.rem(value + n, n)

    right, left = (mod(z + 1, NZ) * 4 + yl * 2 + c, t), (mod(z - 1, NZ) * 4 + yl * 2 + c, t)
    beside = (z * 4 + (1 - yl) * 2 + c, t)
    across = (z * 4 + (1 - yl) * 2 + 1 - c, t)
    mate = (z * 4 + yl * 2 + 1 - c, t)
    x_peer = [None] + [(g, mod(x + k, NX) * NYH + yh) for k in range(1, NX)]
    y_peer = [None] + [(g, x * NYH + mod(yh + k, NYH)) for k in range(1, NYH)]

    third, rest = g // 12, g % 12
    perm_to = (12 * third + 4 * (rest % 3) + yh, x * NYH + rest // 3)
    perm_from = (12 * third + 3 * yh + rest // 4, x * NYH + g % 4)
    moves = jnp.logical_or(perm_to[0] != g, perm_to[1] != t)

    def place(head):
        return pl.multiple_of(((head % 2) * 2 + head // 2) * HD, HD)

    own = w.at[z, yl, c]
    load_w = pltpu.make_async_copy(win_hbm, own, local_sem.at[0])
    load_w.start()
    load_v = pltpu.make_async_copy(wout_hbm, piece, local_sem.at[1])
    load_v.start()
    load_l = pltpu.make_async_copy(lat_hbm, lat, local_sem.at[2])
    load_l.start()

    barrier = pltpu.get_barrier_semaphore()
    peers = [right, left, beside, across, mate] + x_peer[1:] + y_peer[1:]
    for peer in peers:
        pl.semaphore_signal(barrier, inc=1, device_id=peer, device_id_type=MESH)

    @pl.when(moves)
    def _():
        pl.semaphore_signal(barrier, inc=1, device_id=perm_to, device_id_type=MESH)
        pl.semaphore_signal(barrier, inc=1, device_id=perm_from, device_id_type=MESH)
        pl.semaphore_wait(barrier, len(peers) + 2)

    @pl.when(jnp.logical_not(moves))
    def _():
        pl.semaphore_wait(barrier, len(peers))

    def remote(src, dst, s, r, to):
        return pltpu.make_async_remote_copy(
            src_ref=src, dst_ref=dst, send_sem=s, recv_sem=r, device_id=to, device_id_type=MESH
        )

    def z_of(k):
        if k == 0:
            return z
        step = (k + 1) // 2
        return mod(z - step, NZ) if k % 2 == 1 else mod(z + step, NZ)

    class Ring:
        def __init__(self, quarter, pair, sems):
            self.quarter, self.pair = quarter, pair
            self.zs, self.zr, self.ys, self.yr, self.cs, self.cr = sems
            self.started = []

        def z_copy(self, way, step, landing):
            gone = step if landing else step - 1
            home = mod(z - gone, NZ) if way == 0 else mod(z + gone, NZ)
            ref = self.quarter(home, yl)
            if step == NZ // 2:
                half = ref.shape[0] // 2
                ref = ref.at[pl.ds(way * half, half)]
            return remote(
                ref, ref, self.zs.at[way, step - 1], self.zr.at[way, step - 1], right if way == 0 else left
            )

        def go(self, copy):
            copy.start()
            self.started.append(copy)

        def z_send(self, way, step):
            self.go(self.z_copy(way, step, False))

        def z_recv(self, way, step):
            self.z_copy(way, step, True).wait_recv()

        def y_copy(self, k, row):
            ref = self.quarter(z_of(k), row)
            return remote(ref, ref, self.ys.at[k], self.yr.at[k], beside)

        def y_send(self, k):
            self.go(self.y_copy(k, yl))

        def c_copy(self, k, core):
            ref = self.pair(z_of(k), core)
            return remote(ref, ref, self.cs.at[k], self.cr.at[k], mate)

        def first(self):
            self.z_send(0, 1)
            self.z_send(1, 1)
            self.y_send(0)

        def step(self, s):
            for way in range(2):
                self.z_recv(way, s)
                if s < NZ // 2:
                    self.z_send(way, s + 1)
                    self.y_send(2 * s - 1 + way)
            if s == NZ // 2:
                self.y_send(NZ - 1)

        def cross(self, s):
            for k in chunks_of(s):
                self.y_copy(k, 1 - yl).wait_recv()
                self.go(self.c_copy(k, c))

        def arrive(self, k):
            self.c_copy(k, 1 - c).wait_recv()

        def drain(self):
            for copy in self.started:
                copy.wait_send()

    ring = Ring(lambda h, row: w.at[h, row, c], lambda h, core: w.at[h, :, core], (wz_s, wz_r, wy_s, wy_r, wc_s, wc_r))

    def v_rows(h):
        return pl.ds(pl.multiple_of(h * RANK, RANK), RANK)

    ring2 = Ring(
        lambda h, row: w2.at[v_rows(h), pl.ds(pl.multiple_of(c * 256 + row * HD, HD), HD)],
        lambda h, core: w2.at[v_rows(h), pl.ds(pl.multiple_of(core * 256, 256), 256)],
        (vz_s, vz_r, vy_s, vy_r, vc_s, vc_r),
    )

    load_w.wait()
    ring.first()

    mine2 = w2.at[v_rows(z), pl.ds(pl.multiple_of(c * 256 + yl * HD, HD), HD)]
    perm = remote(piece, mine2, perm_sem.at[0], perm_sem.at[1], perm_to)
    keep = pltpu.make_async_copy(piece, mine2, local_sem.at[3])
    z_to, yl_to, c_to = perm_to[0] // 4, (perm_to[0] // 2) % 2, perm_to[0] % 2
    there = w2.at[v_rows(z_to), pl.ds(pl.multiple_of(c_to * 256 + yl_to * HD, HD), HD)]
    load_v.wait()

    @pl.when(moves)
    def _():
        remote(piece, there, perm_sem.at[0], perm_sem.at[1], perm_to).start()

    @pl.when(jnp.logical_not(moves))
    def _():
        keep.start()

    text_keys = rms(text[:, :HD].astype(F32), gains[1:2, :]).astype(BF16)
    slots = lax.broadcasted_iota(jnp.int32, (1, text.shape[0]), 1).astype(F32)
    text_bias = jnp.minimum(count[0].astype(F32) - 0.5 - slots, 0.0) * 1e30

    load_l.wait()

    def multiply(k):
        h = z_of(k)
        block = w[pl.ds(h, 1)].reshape(4 * RANK, 3 * HD)
        part_sum = jnp.dot(lat[:, pl.ds(pl.multiple_of(h * 256, 256), 256)], block, preferred_element_type=F32)
        if k == 0:
            acc[...] = part_sum
        else:
            acc[...] += part_sum

    steps = NZ // 2
    for s in range(1, steps + 1):
        ring.step(s)
        if s == 2:

            @pl.when(moves)
            def _():
                perm.wait()

            @pl.when(jnp.logical_not(moves))
            def _():
                keep.wait()

            ring2.first()
        if s >= 3:
            ring2.step(s - 2)
        ring.cross(s - 1)
        if s >= 2:
            for k in chunks_of(s - 2):
                ring.arrive(k)
                multiply(k)
    ring.cross(steps)
    for s in (steps - 1, steps):
        for k in chunks_of(s):
            ring.arrive(k)
            multiply(k)

    kv_started = []

    def kv_send(src, dst, s, r, to):
        remote(src, dst, s, r, to).start()

    def kv_mate(dt, p):
        return kv.at[dt, 1, p], kv.at[dt, 2 * c, p], kc_s.at[dt, p], kc_r.at[dt, p], mate

    def kv_across(dt, p):
        return kv.at[dt, 1, p], kv.at[dt, 2 * yl, p], ky_s.at[dt, p], ky_r.at[dt, p], across

    def kv_time(way, p):
        return kv.at[1, 1, p], kv.at[2 * way, 1, p], kz_s.at[way, p], kz_r.at[way, p], right if way == 0 else left

    later = [z < NZ - 1, z > 0]
    earlier = [z > 0, z < NZ - 1]

    def send_own(p):
        for way in range(2):

            @pl.when(later[way])
            def _(way=way):
                kv_send(*kv_time(way, p))

        @pl.when(inner)
        def _():
            kv_send(*kv_across(1, p))

        kv_send(*kv_mate(1, p))

    kv[1, 1, 0] = rms(acc[:, HD : 2 * HD], gains[1:2, :]).astype(BF16)
    send_own(0)
    kv[1, 1, 1] = acc[:, 2 * HD :].astype(BF16)
    send_own(1)
    ring2.step(5)
    scale = HD ** (-0.5) * 1.4426950408889634
    q[...] = (rms(acc[:, :HD], gains[0:1, :]) * scale).astype(BF16)

    def attend(keys, values, bias=None, start=False):
        for b in range(BLOCKS):
            rows = pl.ds(b * ROWS, ROWS)
            scores = lax.dot_general(q[rows, :], keys, NT, preferred_element_type=F32)
            if bias is not None:
                scores = scores + bias
            top = jnp.max(scores, axis=1, keepdims=True)
            if not start:
                before = m[rows, :1]
                top = jnp.maximum(before, top)
            weights = jnp.exp2(scores - top)
            total = jnp.sum(weights, axis=1, keepdims=True)
            mixed = jnp.dot(weights.astype(BF16), values, preferred_element_type=F32)
            if not start:
                fade = jnp.exp2(before - top)
                total = total + fade * l[rows, :1]
                mixed = mixed + fade * o[rows, :]
            m[rows, :] = jnp.broadcast_to(top, (ROWS, HD))
            l[rows, :] = jnp.broadcast_to(total, (ROWS, HD))
            o[rows, :] = mixed

    attend(text_keys, text[:, HD:], text_bias, start=True)
    attend(kv[1, 1, 0], kv[1, 1, 1])
    ring2.step(6)
    for s in range(steps + 1):
        ring2.cross(s)
    ring.drain()

    for p in range(2):
        for way in range(2):

            @pl.when(earlier[way])
            def _(way=way, p=p):
                ref = kv.at[2 * way, 1, p]
                remote(ref, ref, kz_s.at[way, p], kz_r.at[way, p], right).wait_recv()

                @pl.when(inner)
                def _():
                    kv_send(*kv_across(2 * way, p))

                kv_send(*kv_mate(2 * way, p))

    def take(dt, dh, s, r):
        for p in range(2):
            ref = kv.at[dt, dh, p]
            remote(ref, ref, s.at[dt, p], r.at[dt, p], mate).wait_recv()
        attend(kv[dt, dh, 0], kv[dt, dh, 1])

    from_mate, from_across = 2 - 2 * c, 2 - 2 * yl

    take(1, from_mate, kc_s, kc_r)
    for way in range(2):

        @pl.when(earlier[way])
        def _(way=way):
            attend(kv[2 * way, 1, 0], kv[2 * way, 1, 1])

    @pl.when(inner)
    def _():
        take(1, from_across, ky_s, ky_r)

    for way in range(2):

        @pl.when(earlier[way])
        def _(way=way):
            take(2 * way, from_mate, kc_s, kc_r)

    for k in range(NZ):
        ring2.arrive(k)
    ring2.drain()
    for way in range(2):

        @pl.when(jnp.logical_and(earlier[way], inner))
        def _(way=way):
            take(2 * way, from_across, ky_s, ky_r)

    def att_copy(b, k, head):
        ref = att.at[pl.ds(b * ROWS, ROWS), pl.ds(place(head), HD)]
        return remote(ref, ref, at_s.at[b, k - 1], at_r.at[b, k - 1], y_peer[k])

    def sum_copy(b, k):
        return remote(send.at[k - 1, b], got.at[k - 1, b], rs_s.at[b, k - 1], rs_r.at[b, k - 1], x_peer[k])

    for b in range(BLOCKS):
        rows = pl.ds(b * ROWS, ROWS)
        att[rows, pl.ds(place(yh), HD)] = (o[rows, :] / l[rows, :1]).astype(BF16)
        for k in range(1, NYH):
            att_copy(b, k, yh).start()

    for b in range(BLOCKS):
        for k in range(1, NYH):
            att_copy(b, k, mod(yh - k, NYH)).wait_recv()
        block = att[pl.ds(b * ROWS, ROWS), :]
        for k in (1, 2, 3, 0):
            rows = pl.ds(pl.multiple_of(mod(x + k, NX) * OUT, OUT), OUT)
            term = lax.dot_general(w2[rows, :], block, NT, preferred_element_type=F32)
            if k:
                send[k - 1, b] = term.astype(BF16)
                sum_copy(b, k).start()
            else:
                part[b] = term

    for b in range(BLOCKS):
        total = part[b]
        for k in range(1, NX):
            sum_copy(b, k).wait_recv()
            total = total + got[k - 1, b].astype(F32)
        out[:, pl.ds(b * ROWS, ROWS)] = total.astype(BF16)

    for p in range(2):
        for way in range(2):

            @pl.when(later[way])
            def _(way=way, p=p):
                remote(*kv_time(way, p)).wait_send()

        for dt in range(3):
            there_is = None if dt == 1 else earlier[dt // 2]

            def left_here(dt=dt, p=p):
                remote(*kv_mate(dt, p)).wait_send()

                @pl.when(inner)
                def _():
                    remote(*kv_across(dt, p)).wait_send()

            if there_is is None:
                left_here()
            else:
                pl.when(there_is)(left_here)
    for b in range(BLOCKS):
        for k in range(1, NX):
            sum_copy(b, k).wait_send()
            att_copy(b, k, yh).wait_send()


def local(latents, input_weight, norm_gains, text_pairs, text_count, output_weight):
    vmem, anywhere = pl.BlockSpec(memory_space=pltpu.VMEM), pl.BlockSpec(memory_space=pl.ANY)
    dma = pltpu.SemaphoreType.DMA
    steps = NZ // 2
    ring = [dma((2, steps)), dma((2, steps)), dma((NZ,)), dma((NZ,)), dma((NZ,)), dma((NZ,))]
    halo = [dma((2, 2)), dma((2, 2)), dma((3, 2)), dma((3, 2)), dma((3, 2)), dma((3, 2))]
    turned = pl.pallas_call(
        kernel,
        out_shape=jax.ShapeDtypeStruct((OUT, TILE), BF16),
        in_specs=[anywhere, anywhere, vmem, vmem, pl.BlockSpec(memory_space=pltpu.SMEM), anywhere],
        out_specs=vmem,
        scratch_shapes=[
            pltpu.VMEM((TILE, NZ * 4 * RANK), BF16),
            pltpu.VMEM((NZ, 2, 2, RANK, 3 * HD), BF16),
            pltpu.VMEM((NZ * RANK, NYH * HD), BF16),
            pltpu.VMEM((RANK, HD), BF16),
            pltpu.VMEM((TILE, 3 * HD), F32),
            pltpu.VMEM((TILE, HD), BF16),
            pltpu.VMEM((3, 3, 2, TILE, HD), BF16),
            pltpu.VMEM((TILE, HD), F32),
            pltpu.VMEM((TILE, HD), F32),
            pltpu.VMEM((TILE, HD), F32),
            pltpu.VMEM((TILE, NYH * HD), BF16),
            pltpu.VMEM((BLOCKS, OUT, ROWS), F32),
            pltpu.VMEM((NX - 1, BLOCKS, OUT, ROWS), BF16),
            pltpu.VMEM((NX - 1, BLOCKS, OUT, ROWS), BF16),
            dma((4,)),
            dma((2,)),
            *ring,
            *ring,
            *halo,
            dma((BLOCKS, NYH - 1)),
            dma((BLOCKS, NYH - 1)),
            dma((BLOCKS, NX - 1)),
            dma((BLOCKS, NX - 1)),
        ],
        compiler_params=pltpu.CompilerParams(
            collective_id=0, has_side_effects=True, vmem_limit_bytes=60 * 1024 * 1024
        ),
        name="sublayer",
    )(latents, input_weight, norm_gains, text_pairs, text_count, output_weight.T)
    return turned.T


def solution(mesh):
    placed = (P("grid", None), P("grid", "tp"), P(), P(None, "tp"), P(), P("tp", "grid"))
    return jax.shard_map(
        local, mesh=mesh, in_specs=placed, out_specs=P("grid", "tp"), check_vma=False
    )
```

```python
import functools

import jax
import jax.numpy as jnp
from jax import lax
from jax.experimental import pallas as pl
from jax.experimental.pallas import tpu as pltpu
from jax.sharding import PartitionSpec as P

NZ = 12
NX = 4
NYH = 4
TILE = 384
HD = 128
RANK = 64
BLOCKS = 3
ROWS = TILE // BLOCKS
OUT = 192
EPS = 1e-6
MESH = pl.DeviceIdType.MESH
F32 = jnp.float32
BF16 = jnp.bfloat16


def rms(values, gain):
    return values * lax.rsqrt(jnp.mean(values * values, axis=-1, keepdims=True) + EPS) * gain


ORDER = [0, 2, -2, 1, -1, 4, -4, 3, -3, 5, -5, 6]
PARENT = {1: 0, 2: 0, 3: 2, 4: 2, 5: 4, 6: 4}
EDGES = [2, -2, 1, -1, 4, -4, 3, -3, 5, -5, 6, -6]


def parent(offset):
    return PARENT[offset] if offset > 0 else -PARENT[-offset]


def kernel(
    lat_hbm, win_hbm, gains, text, count, wout_hbm, out,
    lat, w, w2, piece, acc, q, kb, vb, m, l, o, att, part, send, got,
    local_sem, perm_sem,
    wz_s, wz_r, wy_s, wy_r, wc_s, wc_r,
    vz_s, vz_r, v_sem,
    kz_s, kz_r, ky_s, ky_r, kc_s, kc_r,
    at_s, at_r, rs_s, rs_r,
):
    g = lax.axis_index("grid")
    t = lax.axis_index("tp")
    z, yl, c = g // 4, (g // 2) % 2, g % 2
    x, yh = t // NYH, t % NYH
    inner = yl + c == 1

    def mod(value, n):
        return lax.rem(value + n, n)

    z_peer = {k: (mod(z + k, NZ) * 4 + yl * 2 + c, t) for k in (1, -1, 2, -2)}
    slant = [(mod(z + k, NZ) * 4 + (1 - yl) * 2 + 1 - c, t) for k in (1, -1)]
    beside = (z * 4 + (1 - yl) * 2 + c, t)
    across = (z * 4 + (1 - yl) * 2 + 1 - c, t)
    mate = (z * 4 + yl * 2 + 1 - c, t)
    x_peer = [None] + [(g, mod(x + k, NX) * NYH + yh) for k in range(1, NX)]
    y_peer = [None] + [(g, x * NYH + mod(yh + k, NYH)) for k in range(1, NYH)]

    third, rest = g // 12, g % 12
    perm_to = (12 * third + 4 * (rest % 3) + yh, x * NYH + rest // 3)
    perm_from = (12 * third + 3 * yh + rest // 4, x * NYH + g % 4)
    moves = jnp.logical_or(perm_to[0] != g, perm_to[1] != t)

    def place(head):
        return (head % 2) * 2 + head // 2

    own = w.at[z, yl, c]
    load_w = pltpu.make_async_copy(win_hbm, own, local_sem.at[0])
    load_w.start()
    load_v = pltpu.make_async_copy(wout_hbm, piece, local_sem.at[1])
    load_v.start()
    load_l = pltpu.make_async_copy(lat_hbm, lat, local_sem.at[2])
    load_l.start()

    barrier = pltpu.get_barrier_semaphore()
    peers = list(z_peer.values()) + slant + [beside, across, mate] + x_peer[1:] + y_peer[1:]
    for peer in peers:
        pl.semaphore_signal(barrier, inc=1, device_id=peer, device_id_type=MESH)

    @pl.when(moves)
    def _():
        pl.semaphore_signal(barrier, inc=1, device_id=perm_to, device_id_type=MESH)
        pl.semaphore_signal(barrier, inc=1, device_id=perm_from, device_id_type=MESH)
        pl.semaphore_wait(barrier, len(peers) + 2)

    @pl.when(jnp.logical_not(moves))
    def _():
        pl.semaphore_wait(barrier, len(peers))

    def remote(src, dst, s, r, to):
        return pltpu.make_async_remote_copy(
            src_ref=src, dst_ref=dst, send_sem=s, recv_sem=r, device_id=to, device_id_type=MESH
        )

    class Ring:
        def __init__(self, quarter, pair, sems):
            self.quarter, self.pair = quarter, pair
            self.zs, self.zr = sems[:2]
            if pair:
                self.ys, self.yr, self.cs, self.cr = sems[2:]
            self.started = []

        def go(self, copy):
            copy.start()
            self.started.append(copy)

        def z_copy(self, offset, landing):
            at = offset if landing else parent(offset)
            ref = self.quarter(mod(z - at, NZ), yl)
            if abs(offset) == NZ // 2:
                half = ref.shape[0] // 2
                ref = ref.at[pl.ds(half if offset < 0 else 0, half)]
            e = EDGES.index(offset)
            return remote(ref, ref, self.zs.at[e], self.zr.at[e], z_peer[offset - parent(offset)])

        def z_recv(self, offset):
            self.z_copy(offset, True).wait_recv()

        def z_forward(self, at):
            for offset in EDGES:
                if parent(offset) == at and (at or offset) and (at * offset > 0 or at == 0):
                    self.go(self.z_copy(offset, False))

        def y_copy(self, offset, row):
            ref = self.quarter(mod(z - offset, NZ), row)
            e = ORDER.index(offset)
            return remote(ref, ref, self.ys.at[e], self.yr.at[e], beside)

        def c_copy(self, offset, core):
            ref = self.pair(mod(z - offset, NZ), core)
            e = ORDER.index(offset)
            return remote(ref, ref, self.cs.at[e], self.cr.at[e], mate)

        def first(self):
            self.z_forward(0)
            if self.pair:
                self.go(self.y_copy(0, yl))

        def take(self, offset):
            self.z_recv(offset)
            if offset == NZ // 2:
                self.z_recv(-offset)
            self.z_forward(offset)
            if self.pair:
                self.go(self.y_copy(offset, yl))

        def cross(self, offset):
            self.y_copy(offset, 1 - yl).wait_recv()
            self.go(self.c_copy(offset, c))

        def arrive(self, offset):
            self.c_copy(offset, 1 - c).wait_recv()

        def drain(self):
            for copy in self.started:
                copy.wait_send()

    ring = Ring(lambda h, row: w.at[h, row, c], lambda h, core: w.at[h, :, core], (wz_s, wz_r, wy_s, wy_r, wc_s, wc_r))

    def v_rows(h):
        return pl.ds(pl.multiple_of(h * RANK, RANK), RANK)

    ring2 = Ring(lambda h, row: w2.at[2 * c + row, v_rows(h)], None, (vz_s, vz_r))

    def w2_beside(row):
        return remote(w2.at[2 * c + row], w2.at[2 * c + row], v_sem.at[0], v_sem.at[1], beside)

    def w2_mate(core):
        ref = w2.at[pl.ds(2 * core, 2)]
        return remote(ref, ref, v_sem.at[2], v_sem.at[3], mate)

    load_w.wait()
    ring.first()

    mine2 = w2.at[2 * c + yl, v_rows(z)]
    perm = remote(piece, mine2, perm_sem.at[0], perm_sem.at[1], perm_to)
    keep = pltpu.make_async_copy(piece, mine2, local_sem.at[3])
    z_to, yl_to, c_to = perm_to[0] // 4, (perm_to[0] // 2) % 2, perm_to[0] % 2
    there = w2.at[2 * c_to + yl_to, v_rows(z_to)]
    load_v.wait()

    @pl.when(moves)
    def _():
        remote(piece, there, perm_sem.at[0], perm_sem.at[1], perm_to).start()

    @pl.when(jnp.logical_not(moves))
    def _():
        keep.start()

    text_keys = rms(text[:, :HD].astype(F32), gains[1:2, :]).astype(BF16)
    text_values = text[:, HD:].astype(F32).T.astype(BF16)
    slots = lax.broadcasted_iota(jnp.int32, (text.shape[0], 1), 0).astype(F32)
    text_bias = jnp.minimum(count[0].astype(F32) - 0.5 - slots, 0.0) * 1e30

    load_l.wait()

    def multiply(offset):
        h = mod(z - offset, NZ)
        block = w[pl.ds(h, 1)].reshape(4 * RANK, 3 * HD)
        part_sum = jnp.dot(lat[:, pl.ds(pl.multiple_of(h * 256, 256), 256)], block, preferred_element_type=F32)
        if offset == 0:
            acc[...] = part_sum
        else:
            acc[...] += part_sum

    def project(offsets):
        for offset in offsets:
            ring.arrive(offset)
            multiply(offset)

    first, second, third_ = ORDER[1:5], ORDER[5:9], ORDER[9:]
    for offset in first:
        ring.take(offset)
    ring.cross(0)

    @pl.when(moves)
    def _():
        perm.wait()

    @pl.when(jnp.logical_not(moves))
    def _():
        keep.wait()

    ring2.first()
    for offset in second:
        ring.take(offset)
    for offset in first:
        ring2.take(offset)
    for offset in first:
        ring.cross(offset)
    project([0])
    for offset in third_:
        ring.take(offset)
    for offset in second:
        ring2.take(offset)
    for offset in second:
        ring.cross(offset)
    project(first)
    for offset in third_:
        ring.cross(offset)
    project(second)
    project(third_)

    kv_started = []

    def kv_send(src, dst, s, r, to):
        remote(src, dst, s, r, to).start()

    def slot(dt, dh, p):
        return (vb if p else kb).at[dt, dh]

    def kv_mate(dt, p):
        return slot(dt, 1, p), slot(dt, 2 * c, p), kc_s.at[dt, p], kc_r.at[dt, p], mate

    def kv_across(p):
        return slot(1, 1, p), slot(1, 2 * yl, p), ky_s.at[1, p], ky_r.at[1, p], across

    def kv_slant(way, p):
        return slot(1, 1, p), slot(2 * way, 2 * yl, p), ky_s.at[2 * way, p], ky_r.at[2 * way, p], slant[way]

    def kv_time(way, p):
        return slot(1, 1, p), slot(2 * way, 1, p), kz_s.at[way, p], kz_r.at[way, p], z_peer[1 - 2 * way]

    later = [z < NZ - 1, z > 0]
    earlier = [z > 0, z < NZ - 1]

    def send_own(p):
        for way in range(2):

            @pl.when(later[way])
            def _(way=way):
                kv_send(*kv_time(way, p))

        @pl.when(inner)
        def _():
            kv_send(*kv_across(p))

        for way in range(2):

            @pl.when(jnp.logical_and(later[way], inner))
            def _(way=way):
                kv_send(*kv_slant(way, p))

        kv_send(*kv_mate(1, p))

    kb[1, 1] = rms(acc[:, HD : 2 * HD], gains[1:2, :]).astype(BF16)
    send_own(0)
    vb[1, 1] = acc[:, 2 * HD :].T.astype(BF16)
    send_own(1)
    scale = HD ** (-0.5) * 1.4426950408889634
    q[...] = (rms(acc[:, :HD], gains[0:1, :]) * scale).T.astype(BF16)

    def attend(keys, values, bias=None, start=False):
        scores = jnp.dot(keys, q[...], preferred_element_type=F32)
        if bias is not None:
            scores = scores + bias
        top = jnp.max(scores, axis=0, keepdims=True)
        if not start:
            before = m[...]
            top = jnp.maximum(before, top)
        weights = jnp.exp2(scores - top)
        total = jnp.sum(weights, axis=0, keepdims=True)
        mixed = jnp.dot(values, weights.astype(BF16), preferred_element_type=F32)
        if not start:
            fade = jnp.exp2(before - top)
            total = total + fade * l[...]
            mixed = mixed + fade * o[...]
        m[...] = top
        l[...] = total
        o[...] = mixed

    def attend_tile(dt, dh):
        attend(kb[dt, dh], vb[dt, dh])

    attend(text_keys, text_values, text_bias, start=True)
    for offset in third_:
        ring2.take(offset)
    w2_beside(yl).start()
    attend_tile(1, 1)

    for p in range(2):
        for way in range(2):

            @pl.when(earlier[way])
            def _(way=way, p=p):
                ref = slot(2 * way, 1, p)
                remote(ref, ref, kz_s.at[way, p], kz_r.at[way, p], mate).wait_recv()
                kv_send(*kv_mate(2 * way, p))

    def land(dt, dh, s, r):
        for p in range(2):
            ref = slot(dt, dh, p)
            remote(ref, ref, s.at[dt, p], r.at[dt, p], mate).wait_recv()

    from_mate, from_across = 2 - 2 * c, 2 - 2 * yl

    land(1, from_mate, kc_s, kc_r)
    attend_tile(1, from_mate)
    for way in range(2):

        @pl.when(earlier[way])
        def _(way=way):
            attend_tile(2 * way, 1)

    w2_beside(1 - yl).wait_recv()
    w2_mate(c).start()

    @pl.when(inner)
    def _():
        land(1, from_across, ky_s, ky_r)
        attend_tile(1, from_across)

    for way in range(2):

        @pl.when(earlier[way])
        def _(way=way):
            land(2 * way, from_mate, kc_s, kc_r)
            attend_tile(2 * way, from_mate)

    for way in range(2):

        @pl.when(jnp.logical_and(earlier[way], inner))
        def _(way=way):
            land(2 * way, from_across, ky_s, ky_r)
            attend_tile(2 * way, from_across)

    def halo_drain():
        for p in range(2):
            remote(*kv_mate(1, p)).wait_send()

            @pl.when(inner)
            def _(p=p):
                remote(*kv_across(p)).wait_send()

            for way in range(2):

                @pl.when(later[way])
                def _(way=way, p=p):
                    remote(*kv_time(way, p)).wait_send()

                @pl.when(jnp.logical_and(later[way], inner))
                def _(way=way, p=p):
                    remote(*kv_slant(way, p)).wait_send()

                @pl.when(earlier[way])
                def _(way=way, p=p):
                    remote(*kv_mate(2 * way, p)).wait_send()

    def att_copy(b, k, head):
        ref = att.at[b, place(head)]
        return remote(ref, ref, at_s.at[b, k - 1], at_r.at[b, k - 1], y_peer[k])

    def sum_copy(b, k):
        return remote(send.at[k - 1, b], got.at[k - 1, b], rs_s.at[b, k - 1], rs_r.at[b, k - 1], x_peer[k])

    turn = 1.0 / l[...]
    for b in range(BLOCKS):
        rows = pl.ds(b * ROWS, ROWS)
        att[b, place(yh)] = (o[:, rows] * turn[:, b * ROWS : (b + 1) * ROWS]).astype(BF16)
        for k in range(1, NYH):
            att_copy(b, k, yh).start()
    ring.drain()
    ring2.drain()
    w2_beside(yl).wait_send()
    w2_mate(1 - c).wait_recv()
    w2_mate(c).wait_send()
    halo_drain()

    for b in range(BLOCKS):
        for k in range(1, NYH):
            att_copy(b, k, mod(yh - k, NYH)).wait_recv()
        block = att[b].reshape(NYH * HD, ROWS)
        for k in (1, 2, 3, 0):
            rows = pl.ds(pl.multiple_of(mod(x + k, NX) * OUT, OUT), OUT)
            weight = jnp.concatenate([w2[p, rows, :] for p in range(NYH)], axis=1)
            term = jnp.dot(weight, block, preferred_element_type=F32)
            if k:
                send[k - 1, b] = term.astype(BF16)
                sum_copy(b, k).start()
            else:
                part[b] = term

    for b in range(BLOCKS):
        for k in range(1, NYH):
            att_copy(b, k, yh).wait_send()
    for b in range(BLOCKS):
        total = part[b]
        for k in range(1, NX):
            sum_copy(b, k).wait_recv()
            total = total + got[k - 1, b].astype(F32)
        out[:, pl.ds(b * ROWS, ROWS)] = total.astype(BF16)

    for b in range(BLOCKS):
        for k in range(1, NX):
            sum_copy(b, k).wait_send()


def local(latents, input_weight, norm_gains, text_pairs, text_count, output_weight):
    vmem, anywhere = pl.BlockSpec(memory_space=pltpu.VMEM), pl.BlockSpec(memory_space=pl.ANY)
    dma = pltpu.SemaphoreType.DMA
    ring = [dma((NZ,)), dma((NZ,)), dma((NZ,)), dma((NZ,)), dma((NZ,)), dma((NZ,))]
    halo = [dma((2, 2)), dma((2, 2)), dma((3, 2)), dma((3, 2)), dma((3, 2)), dma((3, 2))]
    turned = pl.pallas_call(
        kernel,
        out_shape=jax.ShapeDtypeStruct((OUT, TILE), BF16),
        in_specs=[anywhere, anywhere, vmem, vmem, pl.BlockSpec(memory_space=pltpu.SMEM), anywhere],
        out_specs=vmem,
        scratch_shapes=[
            pltpu.VMEM((TILE, NZ * 4 * RANK), BF16),
            pltpu.VMEM((NZ, 2, 2, RANK, 3 * HD), BF16),
            pltpu.VMEM((NYH, NZ * RANK, HD), BF16),
            pltpu.VMEM((RANK, HD), BF16),
            pltpu.VMEM((TILE, 3 * HD), F32),
            pltpu.VMEM((HD, TILE), BF16),
            pltpu.VMEM((3, 3, TILE, HD), BF16),
            pltpu.VMEM((3, 3, HD, TILE), BF16),
            pltpu.VMEM((1, TILE), F32),
            pltpu.VMEM((1, TILE), F32),
            pltpu.VMEM((HD, TILE), F32),
            pltpu.VMEM((BLOCKS, NYH, HD, ROWS), BF16),
            pltpu.VMEM((BLOCKS, OUT, ROWS), F32),
            pltpu.VMEM((NX - 1, BLOCKS, OUT, ROWS), BF16),
            pltpu.VMEM((NX - 1, BLOCKS, OUT, ROWS), BF16),
            dma((4,)),
            dma((2,)),
            *ring,
            dma((NZ,)),
            dma((NZ,)),
            dma((4,)),
            *halo,
            dma((BLOCKS, NYH - 1)),
            dma((BLOCKS, NYH - 1)),
            dma((BLOCKS, NX - 1)),
            dma((BLOCKS, NX - 1)),
        ],
        compiler_params=pltpu.CompilerParams(
            collective_id=0, has_side_effects=True, vmem_limit_bytes=60 * 1024 * 1024
        ),
        name="sublayer",
    )(latents, input_weight, norm_gains, text_pairs, text_count, output_weight.T)
    return turned.T


def solution(mesh):
    placed = (P("grid", None), P("grid", "tp"), P(), P(None, "tp"), P(), P("tp", "grid"))
    return jax.shard_map(
        local, mesh=mesh, in_specs=placed, out_specs=P("grid", "tp"), check_vma=False
    )
```

```python
import functools

import jax
import jax.numpy as jnp
from jax import lax
from jax.experimental import pallas as pl
from jax.experimental.pallas import tpu as pltpu
from jax.sharding import PartitionSpec as P

NZ = 12
NX = 4
NYH = 4
TILE = 384
HD = 128
RANK = 64
BLOCKS = 3
ROWS = TILE // BLOCKS
OUT = 192
EPS = 1e-6
MESH = pl.DeviceIdType.MESH
F32 = jnp.float32
BF16 = jnp.bfloat16


def rms(values, gain):
    return values * lax.rsqrt(jnp.mean(values * values, axis=-1, keepdims=True) + EPS) * gain


ORDER = [0, 2, -2, 1, -1, 4, -4, 3, -3, 5, -5, 6]
PARENT = {1: 0, 2: 0, 3: 2, 4: 2, 5: 4, 6: 4}
EDGES = [2, -2, 1, -1, 4, -4, 3, -3, 5, -5, 6, -6]


def parent(offset):
    return PARENT[offset] if offset > 0 else -PARENT[-offset]


def kernel(
    lat_hbm, win_hbm, gains, text, count, wout_hbm, out,
    lat, w, w2, piece, acc, q, kb, vb, m, l, o, att, part, send, got,
    local_sem, perm_sem,
    wz_s, wz_r, wy_s, wy_r, wc_s, wc_r,
    vz_s, vz_r, v_sem,
    kz_s, kz_r, ky_s, ky_r, kc_s, kc_r,
    at_s, at_r, rs_s, rs_r,
):
    g = lax.axis_index("grid")
    t = lax.axis_index("tp")
    z, yl, c = g // 4, (g // 2) % 2, g % 2
    x, yh = t // NYH, t % NYH
    inner = yl + c == 1

    def mod(value, n):
        return lax.rem(value + n, n)

    z_peer = {k: (mod(z + k, NZ) * 4 + yl * 2 + c, t) for k in (1, -1, 2, -2)}
    slant = [(mod(z + k, NZ) * 4 + (1 - yl) * 2 + 1 - c, t) for k in (1, -1)]
    beside = (z * 4 + (1 - yl) * 2 + c, t)
    across = (z * 4 + (1 - yl) * 2 + 1 - c, t)
    mate = (z * 4 + yl * 2 + 1 - c, t)
    x_peer = [None] + [(g, mod(x + k, NX) * NYH + yh) for k in range(1, NX)]
    y_peer = [None] + [(g, x * NYH + mod(yh + k, NYH)) for k in range(1, NYH)]

    third, rest = g // 12, g % 12
    perm_to = (12 * third + 4 * (rest % 3) + yh, x * NYH + rest // 3)
    perm_from = (12 * third + 3 * yh + rest // 4, x * NYH + g % 4)
    moves = jnp.logical_or(perm_to[0] != g, perm_to[1] != t)

    def place(head):
        return (head % 2) * 2 + head // 2

    own = w.at[z, yl, c]
    load_w = pltpu.make_async_copy(win_hbm, own, local_sem.at[0])
    load_w.start()
    load_v = pltpu.make_async_copy(wout_hbm, piece, local_sem.at[1])
    load_v.start()
    load_l = pltpu.make_async_copy(lat_hbm, lat, local_sem.at[2])
    load_l.start()

    barrier = pltpu.get_barrier_semaphore()
    peers = list(z_peer.values()) + slant + [beside, across, mate] + x_peer[1:] + y_peer[1:]
    for peer in peers:
        pl.semaphore_signal(barrier, inc=1, device_id=peer, device_id_type=MESH)

    @pl.when(moves)
    def _():
        pl.semaphore_signal(barrier, inc=1, device_id=perm_to, device_id_type=MESH)
        pl.semaphore_signal(barrier, inc=1, device_id=perm_from, device_id_type=MESH)
        pl.semaphore_wait(barrier, len(peers) + 2)

    @pl.when(jnp.logical_not(moves))
    def _():
        pl.semaphore_wait(barrier, len(peers))

    def remote(src, dst, s, r, to):
        return pltpu.make_async_remote_copy(
            src_ref=src, dst_ref=dst, send_sem=s, recv_sem=r, device_id=to, device_id_type=MESH
        )

    class Ring:
        def __init__(self, quarter, pair, sems):
            self.quarter, self.pair = quarter, pair
            self.zs, self.zr = sems[:2]
            if pair:
                self.ys, self.yr, self.cs, self.cr = sems[2:]
            self.started = []

        def go(self, copy):
            copy.start()
            self.started.append(copy)

        def z_copy(self, offset, landing):
            at = offset if landing else parent(offset)
            ref = self.quarter(mod(z - at, NZ), yl)
            if abs(offset) == NZ // 2:
                half = ref.shape[0] // 2
                ref = ref.at[pl.ds(half if offset < 0 else 0, half)]
            e = EDGES.index(offset)
            return remote(ref, ref, self.zs.at[e], self.zr.at[e], z_peer[offset - parent(offset)])

        def z_recv(self, offset):
            self.z_copy(offset, True).wait_recv()

        def z_forward(self, at):
            for offset in EDGES:
                if parent(offset) == at and (at or offset) and (at * offset > 0 or at == 0):
                    self.go(self.z_copy(offset, False))

        def y_copy(self, offset, row):
            ref = self.quarter(mod(z - offset, NZ), row)
            e = ORDER.index(offset)
            return remote(ref, ref, self.ys.at[e], self.yr.at[e], beside)

        def c_copy(self, offset, core):
            ref = self.pair(mod(z - offset, NZ), core)
            e = ORDER.index(offset)
            return remote(ref, ref, self.cs.at[e], self.cr.at[e], mate)

        def first(self):
            self.z_forward(0)
            if self.pair:
                self.go(self.y_copy(0, yl))

        def take(self, offset):
            self.z_recv(offset)
            if offset == NZ // 2:
                self.z_recv(-offset)
            self.z_forward(offset)
            if self.pair:
                self.go(self.y_copy(offset, yl))

        def cross(self, offset):
            self.y_copy(offset, 1 - yl).wait_recv()
            self.go(self.c_copy(offset, c))

        def arrive(self, offset):
            self.c_copy(offset, 1 - c).wait_recv()

        def drain(self):
            for copy in self.started:
                copy.wait_send()

    ring = Ring(lambda h, row: w.at[h, row, c], lambda h, core: w.at[h, :, core], (wz_s, wz_r, wy_s, wy_r, wc_s, wc_r))

    def v_rows(h):
        return pl.ds(pl.multiple_of(h * RANK, RANK), RANK)

    ring2 = Ring(lambda h, row: w2.at[2 * c + row, v_rows(h)], None, (vz_s, vz_r))

    def w2_beside(row):
        return remote(w2.at[2 * c + row], w2.at[2 * c + row], v_sem.at[0], v_sem.at[1], beside)

    def w2_mate(core):
        ref = w2.at[pl.ds(2 * core, 2)]
        return remote(ref, ref, v_sem.at[2], v_sem.at[3], mate)

    load_w.wait()
    ring.first()

    mine2 = w2.at[2 * c + yl, v_rows(z)]
    perm = remote(piece, mine2, perm_sem.at[0], perm_sem.at[1], perm_to)
    keep = pltpu.make_async_copy(piece, mine2, local_sem.at[3])
    z_to, yl_to, c_to = perm_to[0] // 4, (perm_to[0] // 2) % 2, perm_to[0] % 2
    there = w2.at[2 * c_to + yl_to, v_rows(z_to)]
    load_v.wait()

    @pl.when(moves)
    def _():
        remote(piece, there, perm_sem.at[0], perm_sem.at[1], perm_to).start()

    @pl.when(jnp.logical_not(moves))
    def _():
        keep.start()

    text_keys = rms(text[:, :HD].astype(F32), gains[1:2, :]).astype(BF16)
    text_values = text[:, HD:].astype(F32).T.astype(BF16)
    slots = lax.broadcasted_iota(jnp.int32, (text.shape[0], 1), 0).astype(F32)
    text_bias = jnp.minimum(count[0].astype(F32) - 0.5 - slots, 0.0) * 1e30

    load_l.wait()

    def multiply(offset):
        h = mod(z - offset, NZ)
        block = w[pl.ds(h, 1)].reshape(4 * RANK, 3 * HD)
        part_sum = jnp.dot(lat[:, pl.ds(pl.multiple_of(h * 256, 256), 256)], block, preferred_element_type=F32)
        if offset == 0:
            acc[...] = part_sum
        else:
            acc[...] += part_sum

    def project(offsets):
        for offset in offsets:
            ring.arrive(offset)
            multiply(offset)

    first, second, third_ = ORDER[1:5], ORDER[5:9], ORDER[9:]
    for offset in first:
        ring.take(offset)
    ring.cross(0)

    for offset in second:
        ring.take(offset)

    @pl.when(moves)
    def _():
        perm.wait()

    @pl.when(jnp.logical_not(moves))
    def _():
        keep.wait()

    ring2.first()
    for offset in first:
        ring.cross(offset)
    project([0])
    for offset in third_:
        ring.take(offset)
    for offset in first:
        ring2.take(offset)
    for offset in second:
        ring.cross(offset)
    project(first)
    for offset in third_:
        ring.cross(offset)
    for offset in second:
        ring2.take(offset)
    project(second)
    project(third_)

    kv_started = []

    def kv_send(src, dst, s, r, to):
        remote(src, dst, s, r, to).start()

    def slot(dt, dh, p):
        return (vb if p else kb).at[dt, dh]

    def kv_mate(dt, p):
        return slot(dt, 1, p), slot(dt, 2 * c, p), kc_s.at[dt, p], kc_r.at[dt, p], mate

    def kv_across(p):
        return slot(1, 1, p), slot(1, 2 * yl, p), ky_s.at[1, p], ky_r.at[1, p], across

    def kv_slant(way, p):
        return slot(1, 1, p), slot(2 * way, 2 * yl, p), ky_s.at[2 * way, p], ky_r.at[2 * way, p], slant[way]

    def kv_time(way, p):
        return slot(1, 1, p), slot(2 * way, 1, p), kz_s.at[way, p], kz_r.at[way, p], z_peer[1 - 2 * way]

    later = [z < NZ - 1, z > 0]
    earlier = [z > 0, z < NZ - 1]

    def send_own(p):
        for way in range(2):

            @pl.when(later[way])
            def _(way=way):
                kv_send(*kv_time(way, p))

        @pl.when(inner)
        def _():
            kv_send(*kv_across(p))

        kv_send(*kv_mate(1, p))

    kb[1, 1] = rms(acc[:, HD : 2 * HD], gains[1:2, :]).astype(BF16)
    send_own(0)
    vb[1, 1] = acc[:, 2 * HD :].T.astype(BF16)
    send_own(1)
    scale = HD ** (-0.5) * 1.4426950408889634
    q[...] = (rms(acc[:, :HD], gains[0:1, :]) * scale).T.astype(BF16)

    def attend(keys, values, bias=None, start=False, at=slice(None)):
        scores = jnp.dot(keys, q[:, at], preferred_element_type=F32)
        if bias is not None:
            scores = scores + bias
        top = jnp.max(scores, axis=0, keepdims=True)
        if not start:
            before = m[:, at]
            top = jnp.maximum(before, top)
        weights = jnp.exp2(scores - top)
        total = jnp.sum(weights, axis=0, keepdims=True)
        mixed = jnp.dot(values, weights.astype(BF16), preferred_element_type=F32)
        if not start:
            fade = jnp.exp2(before - top)
            total = total + fade * l[:, at]
            mixed = mixed + fade * o[:, at]
        m[:, at] = top
        l[:, at] = total
        o[:, at] = mixed

    def attend_tile(dt, dh, at=slice(None)):
        attend(kb[dt, dh], vb[dt, dh], at=at)

    attend(text_keys, text_values, text_bias, start=True)
    for p in range(2):
        for way in range(2):

            @pl.when(jnp.logical_and(later[way], inner))
            def _(way=way, p=p):
                kv_send(*kv_slant(way, p))

    for offset in third_:
        ring2.take(offset)
    w2_beside(yl).start()
    attend_tile(1, 1)

    for p in range(2):
        for way in range(2):

            @pl.when(earlier[way])
            def _(way=way, p=p):
                ref = slot(2 * way, 1, p)
                remote(ref, ref, kz_s.at[way, p], kz_r.at[way, p], mate).wait_recv()
                kv_send(*kv_mate(2 * way, p))

    def land(dt, dh, s, r):
        for p in range(2):
            ref = slot(dt, dh, p)
            remote(ref, ref, s.at[dt, p], r.at[dt, p], mate).wait_recv()

    from_mate, from_across = 2 - 2 * c, 2 - 2 * yl

    land(1, from_mate, kc_s, kc_r)
    attend_tile(1, from_mate)
    for way in range(2):

        @pl.when(earlier[way])
        def _(way=way):
            attend_tile(2 * way, 1)

    w2_beside(1 - yl).wait_recv()
    w2_mate(c).start()

    @pl.when(inner)
    def _():
        land(1, from_across, ky_s, ky_r)
        attend_tile(1, from_across)

    for way in range(2):

        @pl.when(earlier[way])
        def _(way=way):
            land(2 * way, from_mate, kc_s, kc_r)
            attend_tile(2 * way, from_mate)

    for way in range(2):

        @pl.when(jnp.logical_and(earlier[way], inner))
        def _(way=way):
            land(2 * way, from_across, ky_s, ky_r)

    def halo_drain():
        for p in range(2):
            remote(*kv_mate(1, p)).wait_send()

            @pl.when(inner)
            def _(p=p):
                remote(*kv_across(p)).wait_send()

            for way in range(2):

                @pl.when(later[way])
                def _(way=way, p=p):
                    remote(*kv_time(way, p)).wait_send()

                @pl.when(jnp.logical_and(later[way], inner))
                def _(way=way, p=p):
                    remote(*kv_slant(way, p)).wait_send()

                @pl.when(earlier[way])
                def _(way=way, p=p):
                    remote(*kv_mate(2 * way, p)).wait_send()

    def att_copy(b, k, head):
        ref = att.at[b, place(head)]
        return remote(ref, ref, at_s.at[b, k - 1], at_r.at[b, k - 1], y_peer[k])

    def sum_copy(b, k):
        return remote(send.at[k - 1, b], got.at[k - 1, b], rs_s.at[b, k - 1], rs_r.at[b, k - 1], x_peer[k])

    for b in range(BLOCKS):
        rows = pl.ds(b * ROWS, ROWS)
        for way in range(2):

            @pl.when(jnp.logical_and(earlier[way], inner))
            def _(way=way, rows=rows):
                attend_tile(2 * way, from_across, rows)

        att[b, place(yh)] = (o[:, rows] * (1.0 / l[:, rows])).astype(BF16)
        for k in range(1, NYH):
            att_copy(b, k, yh).start()
    ring.drain()
    ring2.drain()
    w2_beside(yl).wait_send()
    w2_mate(1 - c).wait_recv()
    w2_mate(c).wait_send()
    halo_drain()

    for b in range(BLOCKS):
        for k in range(1, NYH):
            att_copy(b, k, mod(yh - k, NYH)).wait_recv()
        block = att[b].reshape(NYH * HD, ROWS)
        for k in (2, 1, 3, 0):
            rows = pl.ds(pl.multiple_of(mod(x + k, NX) * OUT, OUT), OUT)
            weight = jnp.concatenate([w2[p, rows, :] for p in range(NYH)], axis=1)
            term = jnp.dot(weight, block, preferred_element_type=F32)
            if k:
                send[k - 1, b] = term.astype(BF16)
                sum_copy(b, k).start()
            else:
                part[b] = term

    for b in range(BLOCKS):
        for k in range(1, NYH):
            att_copy(b, k, yh).wait_send()
    for b in range(BLOCKS):
        total = part[b]
        for k in range(1, NX):
            sum_copy(b, k).wait_recv()
            total = total + got[k - 1, b].astype(F32)
        out[:, pl.ds(b * ROWS, ROWS)] = total.astype(BF16)

    for b in range(BLOCKS):
        for k in range(1, NX):
            sum_copy(b, k).wait_send()


def local(latents, input_weight, norm_gains, text_pairs, text_count, output_weight):
    vmem, anywhere = pl.BlockSpec(memory_space=pltpu.VMEM), pl.BlockSpec(memory_space=pl.ANY)
    dma = pltpu.SemaphoreType.DMA
    ring = [dma((NZ,)), dma((NZ,)), dma((NZ,)), dma((NZ,)), dma((NZ,)), dma((NZ,))]
    halo = [dma((2, 2)), dma((2, 2)), dma((3, 2)), dma((3, 2)), dma((3, 2)), dma((3, 2))]
    turned = pl.pallas_call(
        kernel,
        out_shape=jax.ShapeDtypeStruct((OUT, TILE), BF16),
        in_specs=[anywhere, anywhere, vmem, vmem, pl.BlockSpec(memory_space=pltpu.SMEM), anywhere],
        out_specs=vmem,
        scratch_shapes=[
            pltpu.VMEM((TILE, NZ * 4 * RANK), BF16),
            pltpu.VMEM((NZ, 2, 2, RANK, 3 * HD), BF16),
            pltpu.VMEM((NYH, NZ * RANK, HD), BF16),
            pltpu.VMEM((RANK, HD), BF16),
            pltpu.VMEM((TILE, 3 * HD), F32),
            pltpu.VMEM((HD, TILE), BF16),
            pltpu.VMEM((3, 3, TILE, HD), BF16),
            pltpu.VMEM((3, 3, HD, TILE), BF16),
            pltpu.VMEM((1, TILE), F32),
            pltpu.VMEM((1, TILE), F32),
            pltpu.VMEM((HD, TILE), F32),
            pltpu.VMEM((BLOCKS, NYH, HD, ROWS), BF16),
            pltpu.VMEM((BLOCKS, OUT, ROWS), F32),
            pltpu.VMEM((NX - 1, BLOCKS, OUT, ROWS), BF16),
            pltpu.VMEM((NX - 1, BLOCKS, OUT, ROWS), BF16),
            dma((4,)),
            dma((2,)),
            *ring,
            dma((NZ,)),
            dma((NZ,)),
            dma((4,)),
            *halo,
            dma((BLOCKS, NYH - 1)),
            dma((BLOCKS, NYH - 1)),
            dma((BLOCKS, NX - 1)),
            dma((BLOCKS, NX - 1)),
        ],
        compiler_params=pltpu.CompilerParams(
            collective_id=0, has_side_effects=True, vmem_limit_bytes=60 * 1024 * 1024
        ),
        name="sublayer",
    )(latents, input_weight, norm_gains, text_pairs, text_count, output_weight.T)
    return turned.T


def solution(mesh):
    placed = (P("grid", None), P("grid", "tp"), P(), P(None, "tp"), P(), P("tp", "grid"))
    return jax.shard_map(
        local, mesh=mesh, in_specs=placed, out_specs=P("grid", "tp"), check_vma=False
    )
```

```python
import functools

import jax
import jax.numpy as jnp
from jax import lax
from jax.experimental import pallas as pl
from jax.experimental.pallas import tpu as pltpu
from jax.sharding import PartitionSpec as P

NZ = 12
NX = 4
NYH = 4
TILE = 384
HD = 128
RANK = 64
BLOCKS = 3
ROWS = TILE // BLOCKS
OUT = 192
EPS = 1e-6
MESH = pl.DeviceIdType.MESH
F32 = jnp.float32
BF16 = jnp.bfloat16


def rms(values, gain):
    return values * lax.rsqrt(jnp.mean(values * values, axis=-1, keepdims=True) + EPS) * gain


ORDER = [0, 2, -2, 1, -1, 4, -4, 3, -3, 5, -5, 6]
PARENT = {1: 0, 2: 0, 3: 2, 4: 2, 5: 4, 6: 4}
EDGES = [2, -2, 1, -1, 4, -4, 3, -3, 5, -5, 6, -6]


def parent(offset):
    return PARENT[offset] if offset > 0 else -PARENT[-offset]


def kernel(
    lat_hbm, win_hbm, gains, text, count, wout_hbm, out,
    lat, w, w2, piece, acc, q, kb, vb, m, l, o, att, part, send, got,
    local_sem, perm_sem,
    wz_s, wz_r, wy_s, wy_r, wc_s, wc_r,
    vz_s, vz_r, v_sem,
    kz_s, kz_r, ky_s, ky_r, kc_s, kc_r,
    at_s, at_r, rs_s, rs_r,
):
    g = lax.axis_index("grid")
    t = lax.axis_index("tp")
    z, yl, c = g // 4, (g // 2) % 2, g % 2
    x, yh = t // NYH, t % NYH
    inner = yl + c == 1

    def mod(value, n):
        return lax.rem(value + n, n)

    z_peer = {k: (mod(z + k, NZ) * 4 + yl * 2 + c, t) for k in (1, -1, 2, -2)}
    slant = [(mod(z + k, NZ) * 4 + (1 - yl) * 2 + 1 - c, t) for k in (1, -1)]
    beside = (z * 4 + (1 - yl) * 2 + c, t)
    across = (z * 4 + (1 - yl) * 2 + 1 - c, t)
    mate = (z * 4 + yl * 2 + 1 - c, t)
    x_peer = [None] + [(g, mod(x + k, NX) * NYH + yh) for k in range(1, NX)]
    y_peer = [None] + [(g, x * NYH + mod(yh + k, NYH)) for k in range(1, NYH)]

    third, rest = g // 12, g % 12
    perm_to = (12 * third + 4 * (rest % 3) + yh, x * NYH + rest // 3)
    perm_from = (12 * third + 3 * yh + rest // 4, x * NYH + g % 4)
    moves = jnp.logical_or(perm_to[0] != g, perm_to[1] != t)

    def place(head):
        return (head % 2) * 2 + head // 2

    own = w.at[z, yl, c]
    load_w = pltpu.make_async_copy(win_hbm, own, local_sem.at[0])
    load_w.start()
    load_v = pltpu.make_async_copy(wout_hbm, piece, local_sem.at[1])
    load_v.start()
    load_l = pltpu.make_async_copy(lat_hbm, lat, local_sem.at[2])
    load_l.start()

    barrier = pltpu.get_barrier_semaphore()
    peers = list(z_peer.values()) + slant + [beside, across, mate] + x_peer[1:] + y_peer[1:]
    for peer in peers:
        pl.semaphore_signal(barrier, inc=1, device_id=peer, device_id_type=MESH)

    @pl.when(moves)
    def _():
        pl.semaphore_signal(barrier, inc=1, device_id=perm_to, device_id_type=MESH)
        pl.semaphore_signal(barrier, inc=1, device_id=perm_from, device_id_type=MESH)
        pl.semaphore_wait(barrier, len(peers) + 2)

    @pl.when(jnp.logical_not(moves))
    def _():
        pl.semaphore_wait(barrier, len(peers))

    def remote(src, dst, s, r, to):
        return pltpu.make_async_remote_copy(
            src_ref=src, dst_ref=dst, send_sem=s, recv_sem=r, device_id=to, device_id_type=MESH
        )

    class Ring:
        def __init__(self, quarter, pair, sems):
            self.quarter, self.pair = quarter, pair
            self.zs, self.zr = sems[:2]
            if pair:
                self.ys, self.yr, self.cs, self.cr = sems[2:]
            self.started = []

        def go(self, copy):
            copy.start()
            self.started.append(copy)

        def z_copy(self, offset, landing):
            at = offset if landing else parent(offset)
            ref = self.quarter(mod(z - at, NZ), yl)
            if abs(offset) == NZ // 2:
                half = ref.shape[0] // 2
                ref = ref.at[pl.ds(half if offset < 0 else 0, half)]
            e = EDGES.index(offset)
            return remote(ref, ref, self.zs.at[e], self.zr.at[e], z_peer[offset - parent(offset)])

        def z_recv(self, offset):
            self.z_copy(offset, True).wait_recv()

        def z_forward(self, at):
            for offset in EDGES:
                if parent(offset) == at and (at or offset) and (at * offset > 0 or at == 0):
                    self.go(self.z_copy(offset, False))

        def y_copy(self, offset, row):
            ref = self.quarter(mod(z - offset, NZ), row)
            e = ORDER.index(offset)
            return remote(ref, ref, self.ys.at[e], self.yr.at[e], beside)

        def c_copy(self, offset, core):
            ref = self.pair(mod(z - offset, NZ), core)
            e = ORDER.index(offset)
            return remote(ref, ref, self.cs.at[e], self.cr.at[e], mate)

        def first(self):
            self.z_forward(0)
            if self.pair:
                self.go(self.y_copy(0, yl))

        def take(self, offset):
            self.z_recv(offset)
            if offset == NZ // 2:
                self.z_recv(-offset)
            self.z_forward(offset)
            if self.pair:
                self.go(self.y_copy(offset, yl))

        def cross(self, offset):
            self.y_copy(offset, 1 - yl).wait_recv()
            self.go(self.c_copy(offset, c))

        def arrive(self, offset):
            self.c_copy(offset, 1 - c).wait_recv()

        def drain(self):
            for copy in self.started:
                copy.wait_send()

    ring = Ring(lambda h, row: w.at[h, row, c], lambda h, core: w.at[h, :, core], (wz_s, wz_r, wy_s, wy_r, wc_s, wc_r))

    def v_rows(h):
        return pl.ds(pl.multiple_of(h * RANK, RANK), RANK)

    ring2 = Ring(lambda h, row: w2.at[2 * c + row, v_rows(h)], None, (vz_s, vz_r))

    def w2_beside(row):
        return remote(w2.at[2 * c + row], w2.at[2 * c + row], v_sem.at[0], v_sem.at[1], beside)

    def w2_mate(core):
        ref = w2.at[pl.ds(2 * core, 2)]
        return remote(ref, ref, v_sem.at[2], v_sem.at[3], mate)

    load_w.wait()
    ring.first()

    mine2 = w2.at[2 * c + yl, v_rows(z)]
    perm = remote(piece, mine2, perm_sem.at[0], perm_sem.at[1], perm_to)
    keep = pltpu.make_async_copy(piece, mine2, local_sem.at[3])
    z_to, yl_to, c_to = perm_to[0] // 4, (perm_to[0] // 2) % 2, perm_to[0] % 2
    there = w2.at[2 * c_to + yl_to, v_rows(z_to)]
    load_v.wait()

    @pl.when(moves)
    def _():
        remote(piece, there, perm_sem.at[0], perm_sem.at[1], perm_to).start()

    @pl.when(jnp.logical_not(moves))
    def _():
        keep.start()

    text_keys = rms(text[:, :HD].astype(F32), gains[1:2, :]).astype(BF16)
    text_values = text[:, HD:].astype(F32).T.astype(BF16)
    slots = lax.broadcasted_iota(jnp.int32, (text.shape[0], 1), 0).astype(F32)
    text_bias = jnp.minimum(count[0].astype(F32) - 0.5 - slots, 0.0) * 1e30

    load_l.wait()

    def multiply(offset):
        h = mod(z - offset, NZ)
        block = w[pl.ds(h, 1)].reshape(4 * RANK, 3 * HD)
        part_sum = jnp.dot(lat[:, pl.ds(pl.multiple_of(h * 256, 256), 256)], block, preferred_element_type=F32)
        if offset == 0:
            acc[...] = part_sum
        else:
            acc[...] += part_sum

    def project(offsets):
        for offset in offsets:
            ring.arrive(offset)
            multiply(offset)

    first, second, third_ = ORDER[1:5], ORDER[5:9], ORDER[9:]
    for offset in first:
        ring.take(offset)
    ring.cross(0)

    for offset in second:
        ring.take(offset)

    @pl.when(moves)
    def _():
        perm.wait()

    @pl.when(jnp.logical_not(moves))
    def _():
        keep.wait()

    ring2.first()
    for offset in first:
        ring.cross(offset)
    project([0])
    for offset in third_:
        ring.take(offset)
    for offset in first:
        ring2.take(offset)
    for offset in second:
        ring.cross(offset)
    project(first)
    for offset in third_:
        ring.cross(offset)
    for offset in second:
        ring2.take(offset)
    project(second)
    project(third_)

    kv_started = []

    def kv_send(src, dst, s, r, to):
        remote(src, dst, s, r, to).start()

    def slot(dt, dh, p):
        return (vb if p else kb).at[dt, dh]

    def kv_mate(dt, p):
        return slot(dt, 1, p), slot(dt, 2 * c, p), kc_s.at[dt, p], kc_r.at[dt, p], mate

    def kv_across(p):
        return slot(1, 1, p), slot(1, 2 * yl, p), ky_s.at[1, p], ky_r.at[1, p], across

    def kv_slant(way, p):
        return slot(1, 1, p), slot(2 * way, 2 * yl, p), ky_s.at[2 * way, p], ky_r.at[2 * way, p], slant[way]

    def kv_time(way, p):
        return slot(1, 1, p), slot(2 * way, 1, p), kz_s.at[way, p], kz_r.at[way, p], z_peer[1 - 2 * way]

    later = [z < NZ - 1, z > 0]
    earlier = [z > 0, z < NZ - 1]

    def send_own(p):
        for way in range(2):

            @pl.when(later[way])
            def _(way=way):
                kv_send(*kv_time(way, p))

        @pl.when(inner)
        def _():
            kv_send(*kv_across(p))

        kv_send(*kv_mate(1, p))

    kb[1, 1] = rms(acc[:, HD : 2 * HD], gains[1:2, :]).astype(BF16)
    send_own(0)
    vb[1, 1] = acc[:, 2 * HD :].T.astype(BF16)
    send_own(1)
    scale = HD ** (-0.5) * 1.4426950408889634
    q[...] = (rms(acc[:, :HD], gains[0:1, :]) * scale).T.astype(BF16)

    def attend(tiles, start=False):
        scores = []
        for keys, _, bias in tiles:
            these = jnp.dot(keys, q[...], preferred_element_type=F32)
            scores.append(these if bias is None else these + bias)
        tops = [jnp.max(these, axis=0, keepdims=True) for these in scores]
        if not start:
            tops.append(m[...])
        top = functools.reduce(jnp.maximum, tops)
        if not start:
            fade = jnp.exp2(m[...] - top)
            total, mixed = fade * l[...], fade * o[...]
        else:
            total, mixed = 0.0, 0.0
        for these, (_, values, _) in zip(scores, tiles):
            weights = jnp.exp2(these - top)
            total = total + jnp.sum(weights, axis=0, keepdims=True)
            mixed = mixed + jnp.dot(values, weights.astype(BF16), preferred_element_type=F32)
        m[...] = top
        l[...] = total
        o[...] = mixed

    def tile(dt, dh):
        return kb[dt, dh], vb[dt, dh], None

    def attend_times(dh, where=None):
        both = jnp.logical_and(earlier[0], earlier[1])
        cases = [(both, (0, 2))] + [(jnp.logical_not(earlier[1 - way]), (2 * way,)) for way in range(2)]
        for case, times in cases:

            @pl.when(case if where is None else jnp.logical_and(case, where))
            def _(times=times):
                attend([tile(dt, dh) for dt in times])

    attend([(text_keys, text_values, text_bias), tile(1, 1)], start=True)
    for p in range(2):
        for way in range(2):

            @pl.when(jnp.logical_and(later[way], inner))
            def _(way=way, p=p):
                kv_send(*kv_slant(way, p))

    for offset in third_:
        ring2.take(offset)
    w2_beside(yl).start()

    def land(dt, dh, s, r):
        for p in range(2):
            ref = slot(dt, dh, p)
            remote(ref, ref, s.at[dt, p], r.at[dt, p], mate).wait_recv()

    from_mate, from_across = 2 - 2 * c, 2 - 2 * yl

    land(1, from_mate, kc_s, kc_r)
    attend([tile(1, from_mate)])

    for p in range(2):
        for way in range(2):

            @pl.when(earlier[way])
            def _(way=way, p=p):
                ref = slot(2 * way, 1, p)
                remote(ref, ref, kz_s.at[way, p], kz_r.at[way, p], mate).wait_recv()
                kv_send(*kv_mate(2 * way, p))

    attend_times(1)
    w2_beside(1 - yl).wait_recv()
    w2_mate(c).start()

    @pl.when(inner)
    def _():
        land(1, from_across, ky_s, ky_r)
        attend([tile(1, from_across)])

    for way in range(2):

        @pl.when(earlier[way])
        def _(way=way):
            land(2 * way, from_mate, kc_s, kc_r)

    attend_times(from_mate)

    for way in range(2):

        @pl.when(jnp.logical_and(earlier[way], inner))
        def _(way=way):
            land(2 * way, from_across, ky_s, ky_r)

    attend_times(from_across, inner)

    def halo_drain():
        for p in range(2):
            remote(*kv_mate(1, p)).wait_send()

            @pl.when(inner)
            def _(p=p):
                remote(*kv_across(p)).wait_send()

            for way in range(2):

                @pl.when(later[way])
                def _(way=way, p=p):
                    remote(*kv_time(way, p)).wait_send()

                @pl.when(jnp.logical_and(later[way], inner))
                def _(way=way, p=p):
                    remote(*kv_slant(way, p)).wait_send()

                @pl.when(earlier[way])
                def _(way=way, p=p):
                    remote(*kv_mate(2 * way, p)).wait_send()

    def att_copy(b, k, head):
        ref = att.at[b, place(head)]
        return remote(ref, ref, at_s.at[b, k - 1], at_r.at[b, k - 1], y_peer[k])

    def sum_copy(b, k):
        return remote(send.at[k - 1, b], got.at[k - 1, b], rs_s.at[b, k - 1], rs_r.at[b, k - 1], x_peer[k])

    for b in range(BLOCKS):
        rows = pl.ds(b * ROWS, ROWS)
        att[b, place(yh)] = (o[:, rows] * (1.0 / l[:, rows])).astype(BF16)
        for k in range(1, NYH):
            att_copy(b, k, yh).start()
    ring.drain()
    ring2.drain()
    w2_beside(yl).wait_send()
    w2_mate(1 - c).wait_recv()
    w2_mate(c).wait_send()
    halo_drain()

    for b in range(BLOCKS):
        for k in range(1, NYH):
            att_copy(b, k, mod(yh - k, NYH)).wait_recv()
        block = att[b].reshape(NYH * HD, ROWS)
        for k in (2, 1, 3, 0):
            rows = pl.ds(pl.multiple_of(mod(x + k, NX) * OUT, OUT), OUT)
            weight = jnp.concatenate([w2[p, rows, :] for p in range(NYH)], axis=1)
            term = jnp.dot(weight, block, preferred_element_type=F32)
            if k:
                send[k - 1, b] = term.astype(BF16)
                sum_copy(b, k).start()
            else:
                part[b] = term

    for b in range(BLOCKS):
        for k in range(1, NYH):
            att_copy(b, k, yh).wait_send()
    for b in range(BLOCKS):
        total = part[b]
        for k in range(1, NX):
            sum_copy(b, k).wait_recv()
            total = total + got[k - 1, b].astype(F32)
        out[:, pl.ds(b * ROWS, ROWS)] = total.astype(BF16)

    for b in range(BLOCKS):
        for k in range(1, NX):
            sum_copy(b, k).wait_send()


def local(latents, input_weight, norm_gains, text_pairs, text_count, output_weight):
    vmem, anywhere = pl.BlockSpec(memory_space=pltpu.VMEM), pl.BlockSpec(memory_space=pl.ANY)
    dma = pltpu.SemaphoreType.DMA
    ring = [dma((NZ,)), dma((NZ,)), dma((NZ,)), dma((NZ,)), dma((NZ,)), dma((NZ,))]
    halo = [dma((2, 2)), dma((2, 2)), dma((3, 2)), dma((3, 2)), dma((3, 2)), dma((3, 2))]
    turned = pl.pallas_call(
        kernel,
        out_shape=jax.ShapeDtypeStruct((OUT, TILE), BF16),
        in_specs=[anywhere, anywhere, vmem, vmem, pl.BlockSpec(memory_space=pltpu.SMEM), anywhere],
        out_specs=vmem,
        scratch_shapes=[
            pltpu.VMEM((TILE, NZ * 4 * RANK), BF16),
            pltpu.VMEM((NZ, 2, 2, RANK, 3 * HD), BF16),
            pltpu.VMEM((NYH, NZ * RANK, HD), BF16),
            pltpu.VMEM((RANK, HD), BF16),
            pltpu.VMEM((TILE, 3 * HD), F32),
            pltpu.VMEM((HD, TILE), BF16),
            pltpu.VMEM((3, 3, TILE, HD), BF16),
            pltpu.VMEM((3, 3, HD, TILE), BF16),
            pltpu.VMEM((1, TILE), F32),
            pltpu.VMEM((1, TILE), F32),
            pltpu.VMEM((HD, TILE), F32),
            pltpu.VMEM((BLOCKS, NYH, HD, ROWS), BF16),
            pltpu.VMEM((BLOCKS, OUT, ROWS), F32),
            pltpu.VMEM((NX - 1, BLOCKS, OUT, ROWS), BF16),
            pltpu.VMEM((NX - 1, BLOCKS, OUT, ROWS), BF16),
            dma((4,)),
            dma((2,)),
            *ring,
            dma((NZ,)),
            dma((NZ,)),
            dma((4,)),
            *halo,
            dma((BLOCKS, NYH - 1)),
            dma((BLOCKS, NYH - 1)),
            dma((BLOCKS, NX - 1)),
            dma((BLOCKS, NX - 1)),
        ],
        compiler_params=pltpu.CompilerParams(
            collective_id=0, has_side_effects=True, vmem_limit_bytes=60 * 1024 * 1024
        ),
        name="sublayer",
    )(latents, input_weight, norm_gains, text_pairs, text_count, output_weight.T)
    return turned.T


def solution(mesh):
    placed = (P("grid", None), P("grid", "tp"), P(), P(None, "tp"), P(), P("tp", "grid"))
    return jax.shard_map(
        local, mesh=mesh, in_specs=placed, out_specs=P("grid", "tp"), check_vma=False
    )
```

```python
import functools

import jax
import jax.numpy as jnp
from jax import lax
from jax.experimental import pallas as pl
from jax.experimental.pallas import tpu as pltpu
from jax.sharding import PartitionSpec as P

NZ = 12
NX = 4
NYH = 4
TILE = 384
HD = 128
RANK = 64
BLOCKS = 3
ROWS = TILE // BLOCKS
OUT = 192
EPS = 1e-6
MESH = pl.DeviceIdType.MESH
F32 = jnp.float32
BF16 = jnp.bfloat16


def rms(values, gain):
    return values * lax.rsqrt(jnp.mean(values * values, axis=-1, keepdims=True) + EPS) * gain


ORDER = [0, 2, -2, 1, -1, 4, -4, 3, -3, 5, -5, 6]
PARENT = {1: 0, 2: 0, 3: 2, 4: 2, 5: 4, 6: 4}
EDGES = [2, -2, 1, -1, 4, -4, 3, -3, 5, -5, 6, -6]


def parent(offset):
    return PARENT[offset] if offset > 0 else -PARENT[-offset]


def kernel(
    lat_hbm, win_hbm, gains, text, count, wout_hbm, out,
    lat, w, w2, piece, acc, q, kb, vb, m, l, o, att, part, send, got,
    local_sem, perm_sem,
    wz_s, wz_r, wy_s, wy_r, wc_s, wc_r,
    vz_s, vz_r, v_sem,
    kz_s, kz_r, ky_s, ky_r, kc_s, kc_r,
    at_s, at_r, rs_s, rs_r,
):
    g = lax.axis_index("grid")
    t = lax.axis_index("tp")
    z, yl, c = g // 4, (g // 2) % 2, g % 2
    x, yh = t // NYH, t % NYH
    inner = yl + c == 1

    def mod(value, n):
        return lax.rem(value + n, n)

    z_peer = {k: (mod(z + k, NZ) * 4 + yl * 2 + c, t) for k in (1, -1, 2, -2)}
    slant = [(mod(z + k, NZ) * 4 + (1 - yl) * 2 + 1 - c, t) for k in (1, -1)]
    beside = (z * 4 + (1 - yl) * 2 + c, t)
    across = (z * 4 + (1 - yl) * 2 + 1 - c, t)
    mate = (z * 4 + yl * 2 + 1 - c, t)
    x_peer = [None] + [(g, mod(x + k, NX) * NYH + yh) for k in range(1, NX)]
    y_peer = [None] + [(g, x * NYH + mod(yh + k, NYH)) for k in range(1, NYH)]

    third, rest = g // 12, g % 12
    perm_to = (12 * third + 4 * (rest % 3) + yh, x * NYH + rest // 3)
    perm_from = (12 * third + 3 * yh + rest // 4, x * NYH + g % 4)
    moves = jnp.logical_or(perm_to[0] != g, perm_to[1] != t)

    def place(head):
        return (head % 2) * 2 + head // 2

    own = w.at[z, yl, c]
    load_w = pltpu.make_async_copy(win_hbm, own, local_sem.at[0])
    load_w.start()
    load_v = pltpu.make_async_copy(wout_hbm, piece, local_sem.at[1])
    load_v.start()
    load_l = pltpu.make_async_copy(lat_hbm, lat, local_sem.at[2])
    load_l.start()

    barrier = pltpu.get_barrier_semaphore()
    peers = list(z_peer.values()) + slant + [beside, across, mate] + x_peer[1:] + y_peer[1:]
    for peer in peers:
        pl.semaphore_signal(barrier, inc=1, device_id=peer, device_id_type=MESH)

    @pl.when(moves)
    def _():
        pl.semaphore_signal(barrier, inc=1, device_id=perm_to, device_id_type=MESH)
        pl.semaphore_signal(barrier, inc=1, device_id=perm_from, device_id_type=MESH)
        pl.semaphore_wait(barrier, len(peers) + 2)

    @pl.when(jnp.logical_not(moves))
    def _():
        pl.semaphore_wait(barrier, len(peers))

    def remote(src, dst, s, r, to):
        return pltpu.make_async_remote_copy(
            src_ref=src, dst_ref=dst, send_sem=s, recv_sem=r, device_id=to, device_id_type=MESH
        )

    class Ring:
        def __init__(self, quarter, pair, sems):
            self.quarter, self.pair = quarter, pair
            self.zs, self.zr = sems[:2]
            if pair:
                self.ys, self.yr, self.cs, self.cr = sems[2:]
            self.started = []

        def go(self, copy):
            copy.start()
            self.started.append(copy)

        def z_copy(self, offset, landing):
            at = offset if landing else parent(offset)
            ref = self.quarter(mod(z - at, NZ), yl)
            if abs(offset) == NZ // 2:
                half = ref.shape[0] // 2
                ref = ref.at[pl.ds(half if offset < 0 else 0, half)]
            e = EDGES.index(offset)
            return remote(ref, ref, self.zs.at[e], self.zr.at[e], z_peer[offset - parent(offset)])

        def z_recv(self, offset):
            self.z_copy(offset, True).wait_recv()

        def z_forward(self, at):
            for offset in EDGES:
                if parent(offset) == at and (at or offset) and (at * offset > 0 or at == 0):
                    self.go(self.z_copy(offset, False))

        def y_copy(self, offset, row):
            ref = self.quarter(mod(z - offset, NZ), row)
            e = ORDER.index(offset)
            return remote(ref, ref, self.ys.at[e], self.yr.at[e], beside)

        def c_copy(self, offset, core):
            ref = self.pair(mod(z - offset, NZ), core)
            e = ORDER.index(offset)
            return remote(ref, ref, self.cs.at[e], self.cr.at[e], mate)

        def first(self):
            self.z_forward(0)
            if self.pair:
                self.go(self.y_copy(0, yl))

        def take(self, offset):
            self.z_recv(offset)
            if offset == NZ // 2:
                self.z_recv(-offset)
            self.z_forward(offset)
            if self.pair:
                self.go(self.y_copy(offset, yl))

        def cross(self, offset):
            self.y_copy(offset, 1 - yl).wait_recv()
            self.go(self.c_copy(offset, c))

        def arrive(self, offset):
            self.c_copy(offset, 1 - c).wait_recv()

        def drain(self):
            for copy in self.started:
                copy.wait_send()

    ring = Ring(lambda h, row: w.at[h, row, c], lambda h, core: w.at[h, :, core], (wz_s, wz_r, wy_s, wy_r, wc_s, wc_r))

    def v_rows(h):
        return pl.ds(pl.multiple_of(h * RANK, RANK), RANK)

    ring2 = Ring(lambda h, row: w2.at[2 * c + row, v_rows(h)], None, (vz_s, vz_r))

    def w2_beside(row):
        return remote(w2.at[2 * c + row], w2.at[2 * c + row], v_sem.at[0], v_sem.at[1], beside)

    def w2_mate(core):
        ref = w2.at[pl.ds(2 * core, 2)]
        return remote(ref, ref, v_sem.at[2], v_sem.at[3], mate)

    load_w.wait()
    ring.first()

    mine2 = w2.at[2 * c + yl, v_rows(z)]
    perm = remote(piece, mine2, perm_sem.at[0], perm_sem.at[1], perm_to)
    keep = pltpu.make_async_copy(piece, mine2, local_sem.at[3])
    z_to, yl_to, c_to = perm_to[0] // 4, (perm_to[0] // 2) % 2, perm_to[0] % 2
    there = w2.at[2 * c_to + yl_to, v_rows(z_to)]
    load_v.wait()

    @pl.when(moves)
    def _():
        remote(piece, there, perm_sem.at[0], perm_sem.at[1], perm_to).start()

    @pl.when(jnp.logical_not(moves))
    def _():
        keep.start()

    text_keys = rms(text[:, :HD].astype(F32), gains[1:2, :]).astype(BF16)
    text_values = text[:, HD:].astype(F32).T.astype(BF16)
    slots = lax.broadcasted_iota(jnp.int32, (text.shape[0], 1), 0).astype(F32)
    text_bias = jnp.minimum(count[0].astype(F32) - 0.5 - slots, 0.0) * 1e30

    load_l.wait()

    def multiply(offset):
        h = mod(z - offset, NZ)
        block = w[pl.ds(h, 1)].reshape(4 * RANK, 3 * HD)
        part_sum = jnp.dot(lat[:, pl.ds(pl.multiple_of(h * 256, 256), 256)], block, preferred_element_type=F32)
        if offset == 0:
            acc[...] = part_sum
        else:
            acc[...] += part_sum

    def project(offsets):
        for offset in offsets:
            ring.arrive(offset)
            multiply(offset)

    first, second, third_ = ORDER[1:5], ORDER[5:9], ORDER[9:]
    for offset in first:
        ring.take(offset)
    ring.cross(0)

    for offset in second:
        ring.take(offset)

    @pl.when(moves)
    def _():
        perm.wait()

    @pl.when(jnp.logical_not(moves))
    def _():
        keep.wait()

    ring2.first()
    for offset in first:
        ring.cross(offset)
    project([0])
    for offset in third_:
        ring.take(offset)
    for offset in first:
        ring2.take(offset)
    for offset in second:
        ring.cross(offset)
    project(first)
    for offset in third_:
        ring.cross(offset)
    for offset in second:
        ring2.take(offset)
    project(second)
    project(third_)

    kv_started = []

    def kv_send(src, dst, s, r, to):
        remote(src, dst, s, r, to).start()

    def slot(dt, dh, p):
        return (vb if p else kb).at[dt, dh]

    def kv_mate(dt, p):
        return slot(dt, 1, p), slot(dt, 2 * c, p), kc_s.at[dt, p], kc_r.at[dt, p], mate

    def kv_across(p):
        return slot(1, 1, p), slot(1, 2 * yl, p), ky_s.at[1, p], ky_r.at[1, p], across

    def kv_slant(way, p):
        return slot(1, 1, p), slot(2 * way, 2 * yl, p), ky_s.at[2 * way, p], ky_r.at[2 * way, p], slant[way]

    def kv_time(way, p):
        return slot(1, 1, p), slot(2 * way, 1, p), kz_s.at[way, p], kz_r.at[way, p], z_peer[1 - 2 * way]

    later = [z < NZ - 1, z > 0]
    earlier = [z > 0, z < NZ - 1]

    def send_own(p):
        for way in range(2):

            @pl.when(later[way])
            def _(way=way):
                kv_send(*kv_time(way, p))

        @pl.when(inner)
        def _():
            kv_send(*kv_across(p))

        kv_send(*kv_mate(1, p))

    kb[1, 1] = rms(acc[:, HD : 2 * HD], gains[1:2, :]).astype(BF16)
    send_own(0)
    vb[1, 1] = acc[:, 2 * HD :].T.astype(BF16)
    send_own(1)
    scale = HD ** (-0.5) * 1.4426950408889634
    q[...] = (rms(acc[:, :HD], gains[0:1, :]) * scale).T.astype(BF16)

    def attend(tiles, start=False):
        scores = []
        for keys, _, bias in tiles:
            these = jnp.dot(keys, q[...], preferred_element_type=F32)
            scores.append(these if bias is None else these + bias)
        tops = [jnp.max(these, axis=0, keepdims=True) for these in scores]
        if not start:
            tops.append(m[...])
        top = functools.reduce(jnp.maximum, tops)
        if not start:
            fade = jnp.exp2(m[...] - top)
            total, mixed = fade * l[...], fade * o[...]
        else:
            total, mixed = 0.0, 0.0
        for these, (_, values, _) in zip(scores, tiles):
            weights = jnp.exp2(these - top)
            total = total + jnp.sum(weights, axis=0, keepdims=True)
            mixed = mixed + jnp.dot(values, weights.astype(BF16), preferred_element_type=F32)
        m[...] = top
        l[...] = total
        o[...] = mixed

    def tile(dt, dh):
        return kb[dt, dh], vb[dt, dh], None

    def attend_times(heights, where, beside_it=()):
        both = jnp.logical_and(earlier[0], earlier[1])
        cases = [(both, (0, 2))] + [(jnp.logical_not(earlier[1 - way]), (2 * way,)) for way in range(2)]
        for case, times in cases:

            @pl.when(jnp.logical_and(case, where))
            def _(times=times):
                attend([tile(*at) for at in beside_it] + [tile(dt, dh) for dh in heights for dt in times])

    attend([(text_keys, text_values, text_bias), tile(1, 1)], start=True)
    for p in range(2):
        for way in range(2):

            @pl.when(jnp.logical_and(later[way], inner))
            def _(way=way, p=p):
                kv_send(*kv_slant(way, p))

    for offset in third_:
        ring2.take(offset)
    w2_beside(yl).start()

    def land(dt, dh, s, r):
        for p in range(2):
            ref = slot(dt, dh, p)
            remote(ref, ref, s.at[dt, p], r.at[dt, p], mate).wait_recv()

    from_mate, from_across = 2 - 2 * c, 2 - 2 * yl

    land(1, from_mate, kc_s, kc_r)
    attend([tile(1, from_mate)])

    for p in range(2):
        for way in range(2):

            @pl.when(earlier[way])
            def _(way=way, p=p):
                ref = slot(2 * way, 1, p)
                remote(ref, ref, kz_s.at[way, p], kz_r.at[way, p], mate).wait_recv()
                kv_send(*kv_mate(2 * way, p))

    w2_beside(1 - yl).wait_recv()
    w2_mate(c).start()

    @pl.when(inner)
    def _():
        land(1, from_across, ky_s, ky_r)

    outer = jnp.logical_not(inner)
    attend_times([1], inner, [(1, from_across)])
    attend_times([1], outer)

    for way in range(2):

        @pl.when(earlier[way])
        def _(way=way):
            land(2 * way, from_mate, kc_s, kc_r)

    attend_times([from_mate], outer)

    for way in range(2):

        @pl.when(jnp.logical_and(earlier[way], inner))
        def _(way=way):
            land(2 * way, from_across, ky_s, ky_r)

    attend_times([from_mate, from_across], inner)

    def halo_drain():
        for p in range(2):
            remote(*kv_mate(1, p)).wait_send()

            @pl.when(inner)
            def _(p=p):
                remote(*kv_across(p)).wait_send()

            for way in range(2):

                @pl.when(later[way])
                def _(way=way, p=p):
                    remote(*kv_time(way, p)).wait_send()

                @pl.when(jnp.logical_and(later[way], inner))
                def _(way=way, p=p):
                    remote(*kv_slant(way, p)).wait_send()

                @pl.when(earlier[way])
                def _(way=way, p=p):
                    remote(*kv_mate(2 * way, p)).wait_send()

    def att_copy(b, k, head):
        ref = att.at[b, place(head)]
        return remote(ref, ref, at_s.at[b, k - 1], at_r.at[b, k - 1], y_peer[k])

    def sum_copy(b, k):
        return remote(send.at[k - 1, b], got.at[k - 1, b], rs_s.at[b, k - 1], rs_r.at[b, k - 1], x_peer[k])

    for b in range(BLOCKS):
        rows = pl.ds(b * ROWS, ROWS)
        att[b, place(yh)] = (o[:, rows] * (1.0 / l[:, rows])).astype(BF16)
        for k in range(1, NYH):
            att_copy(b, k, yh).start()
    ring.drain()
    ring2.drain()
    w2_beside(yl).wait_send()
    w2_mate(1 - c).wait_recv()
    w2_mate(c).wait_send()
    halo_drain()

    for b in range(BLOCKS):
        for k in range(1, NYH):
            att_copy(b, k, mod(yh - k, NYH)).wait_recv()
        block = att[b].reshape(NYH * HD, ROWS)
        for k in (2, 1, 3, 0):
            rows = pl.ds(pl.multiple_of(mod(x + k, NX) * OUT, OUT), OUT)
            weight = jnp.concatenate([w2[p, rows, :] for p in range(NYH)], axis=1)
            term = jnp.dot(weight, block, preferred_element_type=F32)
            if k:
                send[k - 1, b] = term.astype(BF16)
                sum_copy(b, k).start()
            else:
                part[b] = term

    for b in range(BLOCKS):
        for k in range(1, NYH):
            att_copy(b, k, yh).wait_send()
    for b in range(BLOCKS):
        total = part[b]
        for k in range(1, NX):
            sum_copy(b, k).wait_recv()
            total = total + got[k - 1, b].astype(F32)
        out[:, pl.ds(b * ROWS, ROWS)] = total.astype(BF16)

    for b in range(BLOCKS):
        for k in range(1, NX):
            sum_copy(b, k).wait_send()


def local(latents, input_weight, norm_gains, text_pairs, text_count, output_weight):
    vmem, anywhere = pl.BlockSpec(memory_space=pltpu.VMEM), pl.BlockSpec(memory_space=pl.ANY)
    dma = pltpu.SemaphoreType.DMA
    ring = [dma((NZ,)), dma((NZ,)), dma((NZ,)), dma((NZ,)), dma((NZ,)), dma((NZ,))]
    halo = [dma((2, 2)), dma((2, 2)), dma((3, 2)), dma((3, 2)), dma((3, 2)), dma((3, 2))]
    turned = pl.pallas_call(
        kernel,
        out_shape=jax.ShapeDtypeStruct((OUT, TILE), BF16),
        in_specs=[anywhere, anywhere, vmem, vmem, pl.BlockSpec(memory_space=pltpu.SMEM), anywhere],
        out_specs=vmem,
        scratch_shapes=[
            pltpu.VMEM((TILE, NZ * 4 * RANK), BF16),
            pltpu.VMEM((NZ, 2, 2, RANK, 3 * HD), BF16),
            pltpu.VMEM((NYH, NZ * RANK, HD), BF16),
            pltpu.VMEM((RANK, HD), BF16),
            pltpu.VMEM((TILE, 3 * HD), F32),
            pltpu.VMEM((HD, TILE), BF16),
            pltpu.VMEM((3, 3, TILE, HD), BF16),
            pltpu.VMEM((3, 3, HD, TILE), BF16),
            pltpu.VMEM((1, TILE), F32),
            pltpu.VMEM((1, TILE), F32),
            pltpu.VMEM((HD, TILE), F32),
            pltpu.VMEM((BLOCKS, NYH, HD, ROWS), BF16),
            pltpu.VMEM((BLOCKS, OUT, ROWS), F32),
            pltpu.VMEM((NX - 1, BLOCKS, OUT, ROWS), BF16),
            pltpu.VMEM((NX - 1, BLOCKS, OUT, ROWS), BF16),
            dma((4,)),
            dma((2,)),
            *ring,
            dma((NZ,)),
            dma((NZ,)),
            dma((4,)),
            *halo,
            dma((BLOCKS, NYH - 1)),
            dma((BLOCKS, NYH - 1)),
            dma((BLOCKS, NX - 1)),
            dma((BLOCKS, NX - 1)),
        ],
        compiler_params=pltpu.CompilerParams(
            collective_id=0, has_side_effects=True, vmem_limit_bytes=60 * 1024 * 1024
        ),
        name="sublayer",
    )(latents, input_weight, norm_gains, text_pairs, text_count, output_weight.T)
    return turned.T


def solution(mesh):
    placed = (P("grid", None), P("grid", "tp"), P(), P(None, "tp"), P(), P("tp", "grid"))
    return jax.shard_map(
        local, mesh=mesh, in_specs=placed, out_specs=P("grid", "tp"), check_vma=False
    )
```

```python
import functools

import jax
import jax.numpy as jnp
from jax import lax
from jax.experimental import pallas as pl
from jax.experimental.pallas import tpu as pltpu
from jax.sharding import PartitionSpec as P

NZ = 12
NX = 4
NYH = 4
TILE = 384
HD = 128
RANK = 64
BLOCKS = 3
ROWS = TILE // BLOCKS
OUT = 192
EPS = 1e-6
MESH = pl.DeviceIdType.MESH
F32 = jnp.float32
BF16 = jnp.bfloat16


def rms(values, gain):
    return values * lax.rsqrt(jnp.mean(values * values, axis=-1, keepdims=True) + EPS) * gain


ORDER = [0, 2, -2, 1, -1, 4, -4, 3, -3, 5, -5, 6]
PARENT = {1: 0, 2: 0, 3: 2, 4: 2, 5: 4, 6: 4}
EDGES = [2, -2, 1, -1, 4, -4, 3, -3, 5, -5, 6, -6]


def parent(offset):
    return PARENT[offset] if offset > 0 else -PARENT[-offset]


def kernel(
    lat_hbm, win_hbm, gains, text, count, wout_hbm, out,
    lat, w, w2, piece, acc, q, kb, vb, m, l, o, att, part, send, got,
    local_sem, perm_sem,
    wz_s, wz_r, wy_s, wy_r, wc_s, wc_r,
    vz_s, vz_r, v_sem,
    kz_s, kz_r, ky_s, ky_r, kc_s, kc_r,
    at_s, at_r, rs_s, rs_r,
):
    g = lax.axis_index("grid")
    t = lax.axis_index("tp")
    z, yl, c = g // 4, (g // 2) % 2, g % 2
    x, yh = t // NYH, t % NYH
    inner = yl + c == 1

    def mod(value, n):
        return lax.rem(value + n, n)

    z_peer = {k: (mod(z + k, NZ) * 4 + yl * 2 + c, t) for k in (1, -1, 2, -2)}
    slant = [(mod(z + k, NZ) * 4 + (1 - yl) * 2 + 1 - c, t) for k in (1, -1)]
    beside = (z * 4 + (1 - yl) * 2 + c, t)
    across = (z * 4 + (1 - yl) * 2 + 1 - c, t)
    mate = (z * 4 + yl * 2 + 1 - c, t)
    x_peer = [None] + [(g, mod(x + k, NX) * NYH + yh) for k in range(1, NX)]
    y_peer = [None] + [(g, x * NYH + mod(yh + k, NYH)) for k in range(1, NYH)]

    third, rest = g // 12, g % 12
    perm_to = (12 * third + 4 * (rest % 3) + yh, x * NYH + rest // 3)
    perm_from = (12 * third + 3 * yh + rest // 4, x * NYH + g % 4)
    moves = jnp.logical_or(perm_to[0] != g, perm_to[1] != t)

    def place(head):
        return (head % 2) * 2 + head // 2

    own = w.at[z, yl, c]
    load_w = pltpu.make_async_copy(win_hbm, own, local_sem.at[0])
    load_w.start()
    load_v = pltpu.make_async_copy(wout_hbm, piece, local_sem.at[1])
    load_v.start()
    load_l = pltpu.make_async_copy(lat_hbm, lat, local_sem.at[2])
    load_l.start()

    barrier = pltpu.get_barrier_semaphore()
    peers = list(z_peer.values()) + slant + [beside, across, mate] + x_peer[1:] + y_peer[1:]
    for peer in peers:
        pl.semaphore_signal(barrier, inc=1, device_id=peer, device_id_type=MESH)

    @pl.when(moves)
    def _():
        pl.semaphore_signal(barrier, inc=1, device_id=perm_to, device_id_type=MESH)
        pl.semaphore_signal(barrier, inc=1, device_id=perm_from, device_id_type=MESH)
        pl.semaphore_wait(barrier, len(peers) + 2)

    @pl.when(jnp.logical_not(moves))
    def _():
        pl.semaphore_wait(barrier, len(peers))

    def remote(src, dst, s, r, to):
        return pltpu.make_async_remote_copy(
            src_ref=src, dst_ref=dst, send_sem=s, recv_sem=r, device_id=to, device_id_type=MESH
        )

    class Ring:
        def __init__(self, quarter, pair, sems):
            self.quarter, self.pair = quarter, pair
            self.zs, self.zr = sems[:2]
            if pair:
                self.ys, self.yr, self.cs, self.cr = sems[2:]
            self.started = []

        def go(self, copy):
            copy.start()
            self.started.append(copy)

        def z_copy(self, offset, landing):
            at = offset if landing else parent(offset)
            ref = self.quarter(mod(z - at, NZ), yl)
            if abs(offset) == NZ // 2:
                half = ref.shape[0] // 2
                ref = ref.at[pl.ds(half if offset < 0 else 0, half)]
            e = EDGES.index(offset)
            return remote(ref, ref, self.zs.at[e], self.zr.at[e], z_peer[offset - parent(offset)])

        def z_recv(self, offset):
            self.z_copy(offset, True).wait_recv()

        def z_forward(self, at):
            for offset in EDGES:
                if parent(offset) == at and (at or offset) and (at * offset > 0 or at == 0):
                    self.go(self.z_copy(offset, False))

        def y_copy(self, offset, row):
            ref = self.quarter(mod(z - offset, NZ), row)
            e = ORDER.index(offset)
            return remote(ref, ref, self.ys.at[e], self.yr.at[e], beside)

        def c_copy(self, offset, core):
            ref = self.pair(mod(z - offset, NZ), core)
            e = ORDER.index(offset)
            return remote(ref, ref, self.cs.at[e], self.cr.at[e], mate)

        def first(self):
            self.z_forward(0)
            if self.pair:
                self.go(self.y_copy(0, yl))

        def take(self, offset):
            self.z_recv(offset)
            if offset == NZ // 2:
                self.z_recv(-offset)
            self.z_forward(offset)
            if self.pair:
                self.go(self.y_copy(offset, yl))

        def cross(self, offset):
            self.y_copy(offset, 1 - yl).wait_recv()
            self.go(self.c_copy(offset, c))

        def arrive(self, offset):
            self.c_copy(offset, 1 - c).wait_recv()

        def drain(self):
            for copy in self.started:
                copy.wait_send()

    ring = Ring(lambda h, row: w.at[h, row, c], lambda h, core: w.at[h, :, core], (wz_s, wz_r, wy_s, wy_r, wc_s, wc_r))

    def v_rows(h):
        return pl.ds(pl.multiple_of(h * RANK, RANK), RANK)

    ring2 = Ring(lambda h, row: w2.at[2 * c + row, v_rows(h)], None, (vz_s, vz_r))

    def w2_beside(row):
        return remote(w2.at[2 * c + row], w2.at[2 * c + row], v_sem.at[0], v_sem.at[1], beside)

    def w2_mate(core):
        ref = w2.at[pl.ds(2 * core, 2)]
        return remote(ref, ref, v_sem.at[2], v_sem.at[3], mate)

    load_w.wait()
    ring.first()

    mine2 = w2.at[2 * c + yl, v_rows(z)]
    perm = remote(piece, mine2, perm_sem.at[0], perm_sem.at[1], perm_to)
    keep = pltpu.make_async_copy(piece, mine2, local_sem.at[3])
    z_to, yl_to, c_to = perm_to[0] // 4, (perm_to[0] // 2) % 2, perm_to[0] % 2
    there = w2.at[2 * c_to + yl_to, v_rows(z_to)]
    load_v.wait()

    @pl.when(moves)
    def _():
        remote(piece, there, perm_sem.at[0], perm_sem.at[1], perm_to).start()

    @pl.when(jnp.logical_not(moves))
    def _():
        keep.start()

    text_keys = rms(text[:, :HD].astype(F32), gains[1:2, :]).astype(BF16)
    text_values = text[:, HD:].astype(F32).T.astype(BF16)
    slots = lax.broadcasted_iota(jnp.int32, (text.shape[0], 1), 0).astype(F32)
    text_bias = jnp.minimum(count[0].astype(F32) - 0.5 - slots, 0.0) * 1e30

    load_l.wait()

    def product(offset):
        h = mod(z - offset, NZ)
        block = w[pl.ds(h, 1)].reshape(4 * RANK, 3 * HD)
        return jnp.dot(lat[:, pl.ds(pl.multiple_of(h * 256, 256), 256)], block, preferred_element_type=F32)

    def project(offsets):
        for offset in offsets:
            ring.arrive(offset)
        total = sum(product(offset) for offset in offsets)
        if offsets == [0]:
            acc[...] = total
        else:
            acc[...] += total

    first, second, third_ = ORDER[1:5], ORDER[5:9], ORDER[9:]
    for offset in first:
        ring.take(offset)
    ring.cross(0)

    for offset in second:
        ring.take(offset)

    @pl.when(moves)
    def _():
        perm.wait()

    @pl.when(jnp.logical_not(moves))
    def _():
        keep.wait()

    ring2.first()
    for offset in first:
        ring.cross(offset)
    project([0])
    for offset in third_:
        ring.take(offset)
    for offset in first:
        ring2.take(offset)
    for offset in second:
        ring.cross(offset)
    project(first)
    for offset in third_:
        ring.cross(offset)
    for offset in second:
        ring2.take(offset)
    project(second)
    project(third_)

    kv_started = []

    def kv_send(src, dst, s, r, to):
        remote(src, dst, s, r, to).start()

    def slot(dt, dh, p):
        return (vb if p else kb).at[dt, dh]

    def kv_mate(dt, p):
        return slot(dt, 1, p), slot(dt, 2 * c, p), kc_s.at[dt, p], kc_r.at[dt, p], mate

    def kv_across(p):
        return slot(1, 1, p), slot(1, 2 * yl, p), ky_s.at[1, p], ky_r.at[1, p], across

    def kv_slant(way, p):
        return slot(1, 1, p), slot(2 * way, 2 * yl, p), ky_s.at[2 * way, p], ky_r.at[2 * way, p], slant[way]

    def kv_time(way, p):
        return slot(1, 1, p), slot(2 * way, 1, p), kz_s.at[way, p], kz_r.at[way, p], z_peer[1 - 2 * way]

    later = [z < NZ - 1, z > 0]
    earlier = [z > 0, z < NZ - 1]

    def send_own(p):
        for way in range(2):

            @pl.when(later[way])
            def _(way=way):
                kv_send(*kv_time(way, p))

        @pl.when(inner)
        def _():
            kv_send(*kv_across(p))

        kv_send(*kv_mate(1, p))

    kb[1, 1] = rms(acc[:, HD : 2 * HD], gains[1:2, :]).astype(BF16)
    send_own(0)
    vb[1, 1] = acc[:, 2 * HD :].T.astype(BF16)
    send_own(1)
    scale = HD ** (-0.5) * 1.4426950408889634
    q[...] = (rms(acc[:, :HD], gains[0:1, :]) * scale).T.astype(BF16)

    def attend(tiles, start=False):
        scores = []
        for keys, _, bias in tiles:
            these = jnp.dot(keys, q[...], preferred_element_type=F32)
            scores.append(these if bias is None else these + bias)
        tops = [jnp.max(these, axis=0, keepdims=True) for these in scores]
        if not start:
            tops.append(m[...])
        top = functools.reduce(jnp.maximum, tops)
        if not start:
            fade = jnp.exp2(m[...] - top)
            total, mixed = fade * l[...], fade * o[...]
        else:
            total, mixed = 0.0, 0.0
        for these, (_, values, _) in zip(scores, tiles):
            weights = jnp.exp2(these - top)
            total = total + jnp.sum(weights, axis=0, keepdims=True)
            mixed = mixed + jnp.dot(values, weights.astype(BF16), preferred_element_type=F32)
        m[...] = top
        l[...] = total
        o[...] = mixed

    def tile(dt, dh):
        return kb[dt, dh], vb[dt, dh], None

    def attend_times(dh, where=None):
        both = jnp.logical_and(earlier[0], earlier[1])
        cases = [(both, (0, 2))] + [(jnp.logical_not(earlier[1 - way]), (2 * way,)) for way in range(2)]
        for case, times in cases:

            @pl.when(case if where is None else jnp.logical_and(case, where))
            def _(times=times):
                attend([tile(dt, dh) for dt in times])

    attend([(text_keys, text_values, text_bias), tile(1, 1)], start=True)
    for p in range(2):
        for way in range(2):

            @pl.when(jnp.logical_and(later[way], inner))
            def _(way=way, p=p):
                kv_send(*kv_slant(way, p))

    for offset in third_:
        ring2.take(offset)
    w2_beside(yl).start()

    def land(dt, dh, s, r):
        for p in range(2):
            ref = slot(dt, dh, p)
            remote(ref, ref, s.at[dt, p], r.at[dt, p], mate).wait_recv()

    from_mate, from_across = 2 - 2 * c, 2 - 2 * yl

    land(1, from_mate, kc_s, kc_r)
    attend([tile(1, from_mate)])

    for p in range(2):
        for way in range(2):

            @pl.when(earlier[way])
            def _(way=way, p=p):
                ref = slot(2 * way, 1, p)
                remote(ref, ref, kz_s.at[way, p], kz_r.at[way, p], mate).wait_recv()
                kv_send(*kv_mate(2 * way, p))

    attend_times(1)
    w2_beside(1 - yl).wait_recv()
    w2_mate(c).start()

    @pl.when(inner)
    def _():
        land(1, from_across, ky_s, ky_r)
        attend([tile(1, from_across)])

    for way in range(2):

        @pl.when(earlier[way])
        def _(way=way):
            land(2 * way, from_mate, kc_s, kc_r)

    attend_times(from_mate)

    for way in range(2):

        @pl.when(jnp.logical_and(earlier[way], inner))
        def _(way=way):
            land(2 * way, from_across, ky_s, ky_r)

    attend_times(from_across, inner)

    def halo_drain():
        for p in range(2):
            remote(*kv_mate(1, p)).wait_send()

            @pl.when(inner)
            def _(p=p):
                remote(*kv_across(p)).wait_send()

            for way in range(2):

                @pl.when(later[way])
                def _(way=way, p=p):
                    remote(*kv_time(way, p)).wait_send()

                @pl.when(jnp.logical_and(later[way], inner))
                def _(way=way, p=p):
                    remote(*kv_slant(way, p)).wait_send()

                @pl.when(earlier[way])
                def _(way=way, p=p):
                    remote(*kv_mate(2 * way, p)).wait_send()

    def att_copy(b, k, head):
        ref = att.at[b, place(head)]
        return remote(ref, ref, at_s.at[b, k - 1], at_r.at[b, k - 1], y_peer[k])

    def sum_copy(b, k):
        return remote(send.at[k - 1, b], got.at[k - 1, b], rs_s.at[b, k - 1], rs_r.at[b, k - 1], x_peer[k])

    for b in range(BLOCKS):
        rows = pl.ds(b * ROWS, ROWS)
        att[b, place(yh)] = (o[:, rows] * (1.0 / l[:, rows])).astype(BF16)
        for k in range(1, NYH):
            att_copy(b, k, yh).start()
    ring.drain()
    ring2.drain()
    w2_beside(yl).wait_send()
    w2_mate(1 - c).wait_recv()
    w2_mate(c).wait_send()
    halo_drain()

    for b in range(BLOCKS):
        for k in range(1, NYH):
            att_copy(b, k, mod(yh - k, NYH)).wait_recv()
        block = att[b].reshape(NYH * HD, ROWS)
        for k in (2, 1, 3, 0):
            rows = pl.ds(pl.multiple_of(mod(x + k, NX) * OUT, OUT), OUT)
            weight = jnp.concatenate([w2[p, rows, :] for p in range(NYH)], axis=1)
            term = jnp.dot(weight, block, preferred_element_type=F32)
            if k:
                send[k - 1, b] = term.astype(BF16)
                sum_copy(b, k).start()
            else:
                part[b] = term

    for b in range(BLOCKS):
        for k in range(1, NYH):
            att_copy(b, k, yh).wait_send()
    for b in range(BLOCKS):
        total = part[b]
        for k in range(1, NX):
            sum_copy(b, k).wait_recv()
            total = total + got[k - 1, b].astype(F32)
        out[:, pl.ds(b * ROWS, ROWS)] = total.astype(BF16)

    for b in range(BLOCKS):
        for k in range(1, NX):
            sum_copy(b, k).wait_send()


def local(latents, input_weight, norm_gains, text_pairs, text_count, output_weight):
    vmem, anywhere = pl.BlockSpec(memory_space=pltpu.VMEM), pl.BlockSpec(memory_space=pl.ANY)
    dma = pltpu.SemaphoreType.DMA
    ring = [dma((NZ,)), dma((NZ,)), dma((NZ,)), dma((NZ,)), dma((NZ,)), dma((NZ,))]
    halo = [dma((2, 2)), dma((2, 2)), dma((3, 2)), dma((3, 2)), dma((3, 2)), dma((3, 2))]
    turned = pl.pallas_call(
        kernel,
        out_shape=jax.ShapeDtypeStruct((OUT, TILE), BF16),
        in_specs=[anywhere, anywhere, vmem, vmem, pl.BlockSpec(memory_space=pltpu.SMEM), anywhere],
        out_specs=vmem,
        scratch_shapes=[
            pltpu.VMEM((TILE, NZ * 4 * RANK), BF16),
            pltpu.VMEM((NZ, 2, 2, RANK, 3 * HD), BF16),
            pltpu.VMEM((NYH, NZ * RANK, HD), BF16),
            pltpu.VMEM((RANK, HD), BF16),
            pltpu.VMEM((TILE, 3 * HD), F32),
            pltpu.VMEM((HD, TILE), BF16),
            pltpu.VMEM((3, 3, TILE, HD), BF16),
            pltpu.VMEM((3, 3, HD, TILE), BF16),
            pltpu.VMEM((1, TILE), F32),
            pltpu.VMEM((1, TILE), F32),
            pltpu.VMEM((HD, TILE), F32),
            pltpu.VMEM((BLOCKS, NYH, HD, ROWS), BF16),
            pltpu.VMEM((BLOCKS, OUT, ROWS), F32),
            pltpu.VMEM((NX - 1, BLOCKS, OUT, ROWS), BF16),
            pltpu.VMEM((NX - 1, BLOCKS, OUT, ROWS), BF16),
            dma((4,)),
            dma((2,)),
            *ring,
            dma((NZ,)),
            dma((NZ,)),
            dma((4,)),
            *halo,
            dma((BLOCKS, NYH - 1)),
            dma((BLOCKS, NYH - 1)),
            dma((BLOCKS, NX - 1)),
            dma((BLOCKS, NX - 1)),
        ],
        compiler_params=pltpu.CompilerParams(
            collective_id=0, has_side_effects=True, vmem_limit_bytes=60 * 1024 * 1024
        ),
        name="sublayer",
    )(latents, input_weight, norm_gains, text_pairs, text_count, output_weight.T)
    return turned.T


def solution(mesh):
    placed = (P("grid", None), P("grid", "tp"), P(), P(None, "tp"), P(), P("tp", "grid"))
    return jax.shard_map(
        local, mesh=mesh, in_specs=placed, out_specs=P("grid", "tp"), check_vma=False
    )
```
